32 devices in a mesh: groups: 2 (over x), slab: 16 (over z, y, core).
Axes of the slice: x: 2, y: 2, z: 4, core: 2. Of those that a mesh axis runs over, the one named last changes fastest.
Arguments:
- mode_shapes: float32 [16384, 192], P(('groups', 'slab')), parts along dimension 0, may hold values from -6 to 6
- wall_coupling: float32 [16384, 15], P(('groups', 'slab')), parts along dimension 0, may hold values from -3.5 to 3.5
- owner_dev: int32 [16384, 1], P(('groups', 'slab')), parts along dimension 0, may hold values from 0 to 15; in each aligned block of 512 rows (0 to 511, 512 to 1023, ...) at most 64 rows name the same one
- owner_cell: int32 [16384], P(('groups', 'slab')), parts along dimension 0, may hold values from 0 to 2047
- neighbours: int32 [6, 65536], P(None, ('groups', 'slab')), parts along dimension 1, may hold values from -1 to 32767, as said below
- coupling_blocks: float32 [6, 5, 5, 65536], P(None, None, None, ('groups', 'slab')), parts along dimension 3, may hold values from -0.3 to 0.3
- inv_blocks: float32 [5, 5, 65536], P(None, None, ('groups', 'slab')), parts along dimension 2, may hold values from -0.9 to 3, as said below
Outputs:
- modes_basis: float32 [5, 64, 65536], P(None, None, ('groups', 'slab')), parts along dimension 2
- factor: float32 [128, 64], P('groups'), parts along dimension 0
The draws below stay inside these ranges and needn't reach their ends.
There are 2 independent parts, one for each index of `groups`. The reference program is written for one: setup_inputs(seed, part) draws one part's arguments, and reference() takes and returns one part's arrays. A program takes and returns all parts, laid end to end along the dimension named above; each array names one. Nothing has to cross between parts.
Inputs may be any that keep to these rules, and one draw needn't show every extreme that they name: `owner_dev`: in the rows of one slab device at most 64 shell nodes name the same slab, a bound that some of them reach. `neighbours`: A filled slot of cell c names a cell whose number differs from c by 1 to 256. `inv_blocks`: each block has a positive diagonal entry shared by its five diagonal places and off-diagonal entries of at most 0.3 times it in magnitude.
All inputs are finite; a program needn't handle non-finite values.
Results may differ from the reference program's by a relative error of at most 0.0003.
Values sent between devices are 32-bit elements; how exact they have to be, the bound alone decides.
A program may use at most 192 MiB of HBM per device.

```python
import math
import jax
import jax.numpy as jnp
import numpy as np

VARS = 5
MODES = 64
NBR = 6
SWEEPS = 2
CELL_DEV = 2048
SHELL_DEV = 512
RIM = 256
CAP = 64
CELLS = 32768
SHELL = 8192
N_SLAB = 16


def draw_neighbours(key, part):
    first_key, second_key, third_key = jax.random.split(key, 3)
    numbering = jnp.arange(CELLS, dtype=jnp.int32)
    reach_out = jax.random.randint(first_key, (NBR, CELLS), 1, RIM + 1)
    upward = jax.random.randint(second_key, (NBR, CELLS), 0, 2)
    retained = jax.random.randint(third_key, (NBR, CELLS), 0, 6)
    target = numbering[None, :] + jnp.where(upward == 1, reach_out, -reach_out)
    usable = (target >= 0) & (target < CELLS) & (retained != 0)
    return jnp.where(usable, target, -1).astype(jnp.int32)


def draw_inv_blocks(key, part):
    scale_key, noise_key = jax.random.split(key)
    position = jnp.arange(CELLS, dtype=jnp.float32) / CELLS
    lowest, highest = (0.3, 3.0)
    fraction = jax.random.uniform(scale_key, (CELLS,), jnp.float32)
    scales = jnp.exp(jnp.log(lowest) + fraction * (jnp.log(highest) - jnp.log(lowest)))
    scales = scales * jnp.exp(jnp.log(3.0) * (position - 1.0))
    noise_term = jax.random.uniform(noise_key, (VARS, VARS, CELLS), jnp.float32, -0.3, 0.3)
    identity = jnp.eye(VARS, dtype=jnp.float32)[:, :, None]
    return ((identity + (1.0 - identity) * noise_term) * scales[None, None, :]).astype(jnp.float32)


def set_ends(entries, key, smallest, top_value):
    longest = entries.shape.index(max(entries.shape))
    spots = []
    for shift in (0, 1):
        where = [jax.random.randint(jax.random.fold_in(key, axis), (), 0, length) for axis, length in enumerate(entries.shape)]
        where[longest] = (where[longest] + shift) % entries.shape[longest]
        spots.append(tuple(where))
    return entries.at[spots[0]].set(smallest).at[spots[1]].set(top_value)


def level_of(rng, dims, pieces, least, largest):
    factor_of = 1.0
    for dim, shards_of in pieces:
        draws = jax.random.uniform(jax.random.fold_in(jax.random.fold_in(rng, 6), dim), (shards_of,), jnp.float32, least / len(pieces), largest / len(pieces))
        factor_of = factor_of * jnp.repeat(jnp.exp(draws), dims[dim] // shards_of).reshape((-1,) + (1,) * (len(dims) - 1 - dim))
    return factor_of


def deal_out(key, own, number, rows, amount, top, most, lean):
    sequence = jax.random.permutation(key, amount)
    heavy_load, common = portions_of(amount, rows * top, most, lean, True), portions_of(amount, rows * top, most, lean, False)
    places = jnp.arange(amount)

    def named(sizes, offset_by):
        used = int((sizes > 0).sum())
        fixed = max(1, used // 4)
        moved = fixed + (places - fixed + offset_by * (used - fixed)) % max(1, amount - fixed)
        return jnp.zeros((amount,), jnp.int32).at[sequence[jnp.where(places < fixed, places, moved)]].set(jnp.asarray(sizes, jnp.int32))

    sizes = jnp.where(number % 4 == 0, named(heavy_load, number // 4), named(common, number - number // 4 - 1))
    mixed = jax.random.permutation(jax.random.fold_in(own, 3), amount)
    giver, receiver = mixed[0:amount // 2 * 2:2], mixed[1:amount // 2 * 2:2]
    margin = jnp.minimum(sizes[giver] - 1, most - sizes[receiver]) // 2
    margin = jnp.where((giver == sequence[0]) | (receiver == sequence[0]) | (sizes[receiver] == 0), 0, jnp.maximum(margin, 0))
    moved = jax.random.randint(jax.random.fold_in(own, 4), (amount // 2,), 0, 1 << 20) % (margin + 1)
    sizes = sizes.at[giver].add(-moved).at[receiver].add(moved)
    members = jnp.searchsorted(jnp.cumsum(sizes), jnp.arange(rows * top), side="right").astype(jnp.int32)
    table = members.reshape(top, rows).T
    table = table[jax.random.permutation(jax.random.fold_in(own, 1), rows)]
    offset_by = jax.random.randint(jax.random.fold_in(own, 2), (rows, 1), 0, top)
    return jnp.take_along_axis(table, (jnp.arange(top)[None, :] + offset_by) % top, axis=1)


def portions_of(number_of, total, reach, skew, full):
    portions = [(1 << 20) // math.isqrt(rank ** skew) + 1 for rank in range(1, number_of + 1)]
    largest = reach if full else min(reach, max(-(-total // number_of), total * portions[0] // sum(portions)))
    least = 1 if total - largest >= number_of - 1 else 0
    holding, spare = [largest] + [least] * (number_of - 1), total - largest - least * (number_of - 1)
    while spare > 0:
        free = [i for i in range(1, number_of) if holding[i] < largest] or [i for i in range(1, number_of) if holding[i] < reach]
        whole, left = sum([portions[i] for i in free]), spare
        for i in free:
            extra = min(reach - holding[i], max(1, left * portions[i] // whole), spare)
            holding[i] = holding[i] + extra
            spare = spare - extra
    return np.array(holding)


def scatter_about(rng, dims, deviation, most, pieces=(), kind=jnp.bfloat16):
    array = deviation * jax.random.normal(rng, dims, jnp.float32)
    if pieces:
        array = array * level_of(rng, dims, pieces, -0.22, 0.18)
    return jnp.clip(array, -most, most).astype(kind)


def setup_inputs(seed: int = 0, part: int = 0) -> dict:
    key_of = jax.random.split(jax.random.key(seed), 8)
    part_splits = jax.random.split(jax.random.fold_in(key_of[7], part), 8)
    mode_shapes = scatter_about(part_splits[0], (SHELL, 3 * MODES), 1.0, 6.0, ((0, 16),), jnp.float32)
    wall_coupling = scatter_about(part_splits[1], (SHELL, 3 * VARS), 3 ** -0.5, 3.5, ((0, 16),), jnp.float32)
    owner_dev_keys = jax.random.split(jax.random.fold_in(part_splits[2], 1), SHELL // SHELL_DEV)
    owner_dev_turns = jax.random.permutation(jax.random.fold_in(part_splits[2], 3), SHELL // SHELL_DEV)
    owner_dev = jax.vmap(lambda own, number: deal_out(jax.random.fold_in(part_splits[2], 2), own, number, SHELL_DEV, N_SLAB, 1, CAP, 1))(owner_dev_keys, owner_dev_turns).reshape((SHELL, 1))
    owner_cell = set_ends(jax.random.randint(part_splits[3], (SHELL,), 0, CELL_DEV), jax.random.fold_in(part_splits[3], 1), 0, CELL_DEV - 1).astype(jnp.int32)
    neighbours = draw_neighbours(jax.random.fold_in(jax.random.fold_in(key_of[7], part), 71), part)
    coupling_blocks = scatter_about(part_splits[5], (NBR, VARS, VARS, CELLS), 0.05, 0.3, ((3, 16),), jnp.float32)
    inv_blocks = draw_inv_blocks(jax.random.fold_in(jax.random.fold_in(key_of[7], part), 71), part)
    return dict(mode_shapes=mode_shapes, wall_coupling=wall_coupling, owner_dev=owner_dev, owner_cell=owner_cell, neighbours=neighbours, coupling_blocks=coupling_blocks, inv_blocks=inv_blocks)


def apply_blocks(blocks, field_in):
    rows_out = []
    for out_var in range(field_in.shape[0]):
        summed = blocks[out_var, 0][None, :] * field_in[0]
        for in_var in range(1, field_in.shape[0]):
            summed = summed + blocks[out_var, in_var][None, :] * field_in[in_var]
        rows_out.append(summed)
    return jnp.stack(rows_out)

def couple(weights, shapes):
    node_count = weights.shape[0]
    modes_total = shapes.shape[1] // 3
    weights_split = weights.reshape(node_count, -1, 3)
    shapes_split = shapes.reshape(node_count, 3, modes_total)
    summed = weights_split[:, :, 0, None] * shapes_split[:, None, 0, :]
    for component in range(1, 3):
        summed = summed + weights_split[:, :, component, None] * shapes_split[:, None, component, :]
    return summed.reshape(node_count, -1)

def neighbour_term(field_in, neighbours, coupling_blocks):
    total_cells = field_in.shape[2]
    padded = jnp.concatenate([field_in, jnp.zeros(field_in.shape[:2] + (1,), field_in.dtype)], axis=2)
    safe_ids = jnp.where(neighbours >= 0, neighbours, total_cells).astype(jnp.int32)
    result = jnp.zeros_like(field_in)
    for slot_index in range(NBR):
        gathered = jnp.take(padded, safe_ids[slot_index], axis=2)
        result = result + apply_blocks(coupling_blocks[slot_index], gathered)
    return result

def reference(mode_shapes, wall_coupling, owner_dev, owner_cell, neighbours, coupling_blocks, inv_blocks):
    contribution = couple(wall_coupling, mode_shapes)
    target = (owner_dev[:, 0] * CELL_DEV + owner_cell).astype(jnp.int32)
    forcing = jax.ops.segment_sum(contribution, target, num_segments=CELLS)
    forcing = forcing.T.reshape(VARS, MODES, CELLS)
    state_field = apply_blocks(inv_blocks, forcing)
    for sweep_step in range(SWEEPS):
        state_field = apply_blocks(inv_blocks, forcing - neighbour_term(state_field, neighbours, coupling_blocks))
    matrix = jnp.transpose(state_field, (0, 2, 1)).reshape(VARS * CELLS, MODES)
    basis_out, factor = jnp.linalg.qr(matrix)
    sign_flip = jnp.where(jnp.diagonal(factor) < 0, -1.0, 1.0).astype(factor.dtype)
    basis_out = basis_out * sign_flip[None, :]
    factor = factor * sign_flip[:, None]
    norm_scale = math.sqrt(VARS * CELLS)
    basis_out = jnp.transpose(basis_out.reshape(VARS, CELLS, MODES), (0, 2, 1)) * norm_scale
    return (basis_out, factor / norm_scale)
```

```python
import functools
import math

import jax
import jax.numpy as jnp
from jax import lax
from jax.experimental import pallas as pl
from jax.experimental.pallas import tpu as pltpu
from jax.sharding import PartitionSpec as P

VARS = 5
NBR = 6
COMPS = 3
LANES = 128
TILES = 8
MESH = pl.DeviceIdType.MESH
F32 = jnp.float32
BF16 = jnp.bfloat16


def split_two(value):
    high = value.astype(BF16)
    low = (value - high.astype(F32)).astype(BF16)
    return high, low


def dot_f32(left, right):
    return jnp.dot(left, right, preferred_element_type=F32)


def kernel(
    count, cap, modes, cells, scale,
    payload_ref, dest_ref, nbr_ref, coupling_ref, inv_ref,
    basis_ref, factor_ref,
    outgoing, arrived, loads, tag_rows, hot, scaled, start, first, second, gathered,
    edges, halos, part, sums, whole,
    send_a, recv_a, send_h, recv_h, send_g, recv_g, send_w, recv_w,
):
    me = lax.axis_index("slab")
    nodes = dest_ref.shape[0]
    groups = LANES // cap
    width = modes // groups
    rows = COMPS * width + 16
    tall = VARS * modes
    span = cells // TILES
    step = count // TILES

    def remote(src, dst, send, recv, peer):
        return pltpu.make_async_remote_copy(
            src_ref=src, dst_ref=dst, send_sem=send, recv_sem=recv,
            device_id={"slab": peer}, device_id_type=MESH,
        )

    barrier = pltpu.get_barrier_semaphore()
    for shift in range(1, count):
        pl.semaphore_signal(
            barrier, inc=1, device_id={"slab": lax.rem(me + shift, count)}, device_id_type=MESH
        )
    halos[...] = jnp.zeros_like(halos)

    dest = dest_ref[...]
    lane = lax.broadcasted_iota(jnp.int32, (nodes, LANES), 1)
    names = dest == lane
    earlier = (
        lax.broadcasted_iota(jnp.int32, (nodes, nodes), 1)
        < lax.broadcasted_iota(jnp.int32, (nodes, nodes), 0)
    )
    before = dot_f32(earlier.astype(F32).astype(BF16), names.astype(F32).astype(BF16))
    rank = jnp.sum(jnp.where(names, before, 0.0), axis=1, keepdims=True).astype(jnp.int32)
    place = dest * LANES + rank
    turned = payload_ref[...].T
    pieces = []
    for group in range(groups):
        taken = [
            turned[comp * modes + group * width : comp * modes + (group + 1) * width]
            for comp in range(COMPS)
        ]
        pieces.append(jnp.concatenate(taken + [turned[COMPS * modes : COMPS * modes + 16]], axis=0))
    packed = jnp.concatenate(split_two(jnp.concatenate(pieces, axis=1)), axis=0)

    def pack_for(slab):
        at = place - slab * LANES
        picks = jnp.concatenate(
            [(at + group * cap == lane).astype(F32).astype(BF16) for group in range(groups)], axis=0
        )
        both = dot_f32(packed, picks)
        return both[:rows] + both[rows:]

    pl.semaphore_wait(barrier, count - 1)

    def send_step(shift, carry):
        slab = lax.rem(me + shift, count)
        outgoing[slab] = pack_for(slab)
        remote(outgoing.at[slab], arrived.at[me], send_a.at[slab], recv_a.at[me], slab).start()
        return carry

    lax.fori_loop(1, count, send_step, 0)
    arrived[me] = pack_for(me)

    first_cell = me * cells - span
    window = lax.broadcasted_iota(jnp.int32, (3 * span, span), 0)

    def hot_step(block, carry):
        at = pl.ds(pl.multiple_of(block * span, span), span)
        for slot in range(NBR):
            names_now = nbr_ref[slot : slot + 1, at]
            local = jnp.where(names_now >= 0, names_now - (first_cell + block * span), -1)
            hot[block, :, slot * span : (slot + 1) * span] = (window == local).astype(F32).astype(BF16)
        return carry

    lax.fori_loop(0, TILES, hot_step, 0)

    def scale_step(slot, carry):
        for out_var in range(VARS):
            total = inv_ref[out_var, 0:1, :] * coupling_ref[slot, 0]
            for mid in range(1, VARS):
                total = total + inv_ref[out_var, mid : mid + 1, :] * coupling_ref[slot, mid]
            scaled[slot, out_var] = total
        return carry

    lax.fori_loop(0, NBR, scale_step, 0)

    def arrive_step(shift, carry):
        slab = lax.rem(me + shift, count)
        remote(outgoing.at[slab], arrived.at[slab], send_a.at[slab], recv_a.at[slab], slab).wait()
        return carry

    lax.fori_loop(1, count, arrive_step, 0)

    part_of = lax.broadcasted_iota(jnp.int32, (1, LANES), 1) // cap

    def load_step(bunch, carry):
        at = pl.ds(pl.multiple_of(bunch * LANES, LANES), LANES)
        tags = jnp.zeros((1, LANES), F32)
        built = [[None] * groups for _ in range(VARS)]
        for turn in range(groups):
            here = part_of == turn
            data = arrived[bunch * groups + turn]
            base = COMPS * width
            tags = jnp.where(here, data[base + 15 : base + 16], tags)
            for var in range(VARS):
                load = data[base + COMPS * var : base + COMPS * var + 1] * data[:width]
                for comp in range(1, COMPS):
                    at_row = base + COMPS * var + comp
                    load = load + data[at_row : at_row + 1] * data[comp * width : (comp + 1) * width]
                for group in range(groups):
                    turn_by = ((turn - group) * cap) % LANES
                    moved = pltpu.roll(load, turn_by, 1) if turn_by else load
                    kept = built[var][group]
                    built[var][group] = moved if kept is None else jnp.where(here, moved, kept)
        for var in range(VARS):
            high, low = split_two(jnp.concatenate(built[var], axis=0))
            loads[var * modes : (var + 1) * modes, at] = high
            loads[tall + var * modes : tall + (var + 1) * modes, at] = low
        tag_rows[:, at] = jnp.broadcast_to(tags, (8, LANES))
        return carry

    lax.fori_loop(0, count // groups, load_step, 0)
    tag_column = tag_rows[...].T[:, 0:1].astype(jnp.int32)
    slot_cells = lax.broadcasted_iota(jnp.int32, (count * cap, span), 1)

    def keep(state, block, var, value):
        high, low = split_two(value)
        state[block + 1, var * modes : (var + 1) * modes] = high
        state[block + 1, tall + var * modes : tall + (var + 1) * modes] = low

    def begin(block, side):
        at = pl.ds(pl.multiple_of(block * span, span), span)
        matches = (tag_column == slot_cells + block * span).astype(F32).astype(BF16)
        both = dot_f32(loads[...], matches)
        forcing = both[:tall] + both[tall:]
        for var in range(VARS):
            total = inv_ref[var, 0:1, at] * forcing[:modes]
            for mid in range(1, VARS):
                total = total + inv_ref[var, mid : mid + 1, at] * forcing[mid * modes : (mid + 1) * modes]
            start[block, var * modes : (var + 1) * modes] = total
            keep(first, block, var, total)
            if side is not None:
                edges[0, side, var * modes : (var + 1) * modes] = total

    def sweep(source, target, block, side):
        at = pl.ds(pl.multiple_of(block * span, span), span)
        near = jnp.concatenate([source[block], source[block + 1], source[block + 2]], axis=1)
        for slot in range(NBR):
            both = dot_f32(near, hot[block, :, slot * span : (slot + 1) * span])
            gathered[slot] = both[:tall] + both[tall:]
        for var in range(VARS):
            total = start[block, var * modes : (var + 1) * modes]
            for slot in range(NBR):
                for mid in range(VARS):
                    total = total - (
                        scaled[slot, var, mid : mid + 1, at]
                        * gathered[slot, mid * modes : (mid + 1) * modes]
                    )
            keep(target, block, var, total)
            if side is not None:
                edges[1, side, var * modes : (var + 1) * modes] = total

    def halo_copy(turn, side):
        peer = me - 1 if side == 0 else me + 1
        return remote(
            edges.at[turn, side], halos.at[turn, 1 - side],
            send_h.at[turn, side], recv_h.at[turn, 1 - side], peer,
        )

    def halo_wait(turn, side):
        peer = me - 1 if side == 0 else me + 1
        return remote(
            edges.at[turn, side], halos.at[turn, side],
            send_h.at[turn, side], recv_h.at[turn, side], peer,
        )

    def halo_send(turn):
        @pl.when(me > 0)
        def _():
            halo_copy(turn, 0).start()

        @pl.when(me < count - 1)
        def _():
            halo_copy(turn, 1).start()

    def halo_take(turn, state):
        @pl.when(me > 0)
        def _():
            halo_wait(turn, 0).wait()

        @pl.when(me < count - 1)
        def _():
            halo_wait(turn, 1).wait()

        for side, block in ((0, -1), (1, TILES)):
            for var in range(VARS):
                keep(state, block, var, halos[turn, side, var * modes : (var + 1) * modes])

    last = TILES - 1
    begin(0, 0)
    begin(last, 1)
    halo_send(0)

    def begin_step(block, carry):
        begin(block, None)
        return carry

    lax.fori_loop(1, last, begin_step, 0)

    def first_step(block, carry):
        sweep(first, second, block, None)
        return carry

    def second_step(block, carry):
        sweep(second, first, block, None)
        return carry

    lax.fori_loop(1, TILES // 2, first_step, 0)
    halo_take(0, first)
    sweep(first, second, 0, 0)
    sweep(first, second, last, 1)
    halo_send(1)
    lax.fori_loop(TILES // 2, last, first_step, 0)
    lax.fori_loop(1, last, second_step, 0)
    halo_take(1, second)
    sweep(second, first, 0, None)
    sweep(second, first, last, None)

    def gram_step(block, total):
        for var in range(VARS):
            stack = jnp.concatenate(
                [
                    first[block + 1, var * modes : (var + 1) * modes],
                    first[block + 1, tall + var * modes : tall + (var + 1) * modes],
                ],
                axis=0,
            )
            total = total + lax.dot_general(
                stack, stack, (((1,), (1,)), ((), ())), preferred_element_type=F32
            )
        return total

    gram = lax.fori_loop(0, TILES, gram_step, jnp.zeros((2 * modes, 2 * modes), F32))
    gram = gram[:modes] + gram[modes:]
    gram = gram + pltpu.roll(gram, modes, 1)
    high = modes // TILES
    for tile in range(TILES):
        owner = tile * step
        part[tile] = gram[tile * high : (tile + 1) * high]

        @pl.when(me != owner)
        def _():
            remote(part.at[tile], sums.at[me], send_g.at[tile], recv_g.at[me], owner).start()

        @pl.when(me == owner)
        def _():
            sums[me] = part[tile]

    mine = me // step

    @pl.when(lax.rem(me, step) == 0)
    def _():
        def sum_wait(shift, carry):
            slab = lax.rem(me + shift, count)
            remote(part.at[0], sums.at[slab], send_g.at[0], recv_g.at[slab], slab).wait_recv()
            return carry

        lax.fori_loop(1, count, sum_wait, 0)
        total = sums[0]
        for slab in range(1, count):
            total = total + sums[slab]
        whole[mine] = total
        for shift in range(1, count):
            slab = lax.rem(me + shift, count)
            remote(whole.at[mine], whole.at[mine], send_w.at[slab], recv_w.at[mine], slab).start()

    for tile in range(TILES):
        owner = tile * step

        @pl.when(me != owner)
        def _():
            remote(part.at[tile], sums.at[me], send_g.at[tile], recv_g.at[me], owner).wait_send()
            remote(whole.at[tile], whole.at[tile], send_w.at[0], recv_w.at[tile], owner).wait_recv()

    row_at = lax.broadcasted_iota(jnp.int32, (modes, 2 * modes), 0)
    col_at = lax.broadcasted_iota(jnp.int32, (modes, 2 * modes), 1)
    table = jnp.concatenate([whole[tile] for tile in range(TILES)], axis=0)
    table = jnp.where(col_at < modes, table, jnp.where(col_at - modes == row_at, 1.0, 0.0))
    bands = [table[tile * high : (tile + 1) * high] for tile in range(TILES)]
    inner = lax.broadcasted_iota(jnp.int32, (high, 1), 0)
    for pivot_at in range(modes):
        band, offset = pivot_at // high, pivot_at % high
        row = bands[band][offset : offset + 1]
        row = row * (1.0 / row[:, pivot_at : pivot_at + 1])
        for tile in range(band, TILES):
            column = bands[tile][:, pivot_at : pivot_at + 1]
            if tile == band:
                column = jnp.where(inner > offset, column, 0.0)
            bands[tile] = bands[tile] - column * row
    table = jnp.concatenate(bands, axis=0)
    diagonal = jnp.sum(jnp.where(col_at == row_at, table, 0.0), axis=1, keepdims=True)
    root = jnp.sqrt(diagonal)
    factor_ref[...] = jnp.where(col_at >= row_at, table * (root / diagonal) * (1.0 / scale), 0.0)[:, :modes]
    inverse = pltpu.roll(table * (scale / root), modes, 1)[:, :modes]
    inv_high, inv_low = split_two(inverse)
    mixer = jnp.concatenate([inv_high, inv_high, inv_low], axis=1)

    def basis_step(block, carry):
        at = pl.ds(pl.multiple_of(block * span, span), span)
        for var in range(VARS):
            top = first[block + 1, var * modes : (var + 1) * modes]
            bottom = first[block + 1, tall + var * modes : tall + (var + 1) * modes]
            basis_ref[var, :, at] = dot_f32(mixer, jnp.concatenate([top, bottom, top], axis=0))
        return carry

    lax.fori_loop(0, TILES, basis_step, 0)

    @pl.when(lax.rem(me, step) == 0)
    def _():
        for shift in range(1, count):
            slab = lax.rem(me + shift, count)
            remote(whole.at[mine], whole.at[mine], send_w.at[slab], recv_w.at[mine], slab).wait_send()


def local(
    mode_shapes, wall_coupling, owner_dev, owner_cell, neighbours, coupling_blocks, inv_blocks
):
    count = lax.axis_size("slab")
    cells = inv_blocks.shape[2]
    nodes = mode_shapes.shape[0]
    modes = mode_shapes.shape[1] // COMPS
    cap = max(2, 2 * nodes // count)
    groups = LANES // cap
    rows = COMPS * (modes // groups) + 16
    tall = VARS * modes
    span = cells // TILES
    payload = jnp.concatenate(
        [mode_shapes, wall_coupling, owner_cell.astype(F32)[:, None], jnp.zeros((nodes, 48), F32)], axis=1
    )
    scale = math.sqrt(VARS * cells * count)
    vmem = pl.BlockSpec(memory_space=pltpu.VMEM)
    dma = pltpu.SemaphoreType.DMA
    return pl.pallas_call(
        functools.partial(kernel, count, cap, modes, cells, scale),
        out_shape=(
            jax.ShapeDtypeStruct((VARS, modes, cells), F32),
            jax.ShapeDtypeStruct((modes, modes), F32),
        ),
        in_specs=[vmem] * 5,
        out_specs=(vmem, vmem),
        scratch_shapes=[
            pltpu.VMEM((count, rows, LANES), F32),
            pltpu.VMEM((count, rows, LANES), F32),
            pltpu.VMEM((2 * tall, count * cap), BF16),
            pltpu.VMEM((8, count * cap), F32),
            pltpu.VMEM((TILES, 3 * span, NBR * span), BF16),
            pltpu.VMEM((NBR, VARS, VARS, cells), F32),
            pltpu.VMEM((TILES, tall, span), F32),
            pltpu.VMEM((TILES + 2, 2 * tall, span), BF16),
            pltpu.VMEM((TILES + 2, 2 * tall, span), BF16),
            pltpu.VMEM((NBR, tall, span), F32),
            pltpu.VMEM((2, 2, tall, span), F32),
            pltpu.VMEM((2, 2, tall, span), F32),
            pltpu.VMEM((TILES, modes // TILES, 2 * modes), F32),
            pltpu.VMEM((count, modes // TILES, 2 * modes), F32),
            pltpu.VMEM((TILES, modes // TILES, 2 * modes), F32),
            dma((count,)), dma((count,)), dma((2, 2)), dma((2, 2)),
            dma((TILES,)), dma((count,)), dma((count,)), dma((TILES,)),
        ],
        compiler_params=pltpu.CompilerParams(
            collective_id=0, has_side_effects=True, vmem_limit_bytes=58 * 1024 * 1024
        ),
    )(payload, owner_dev, neighbours, coupling_blocks, inv_blocks)


def solution(mesh):
    in_specs = (
        P(("groups", "slab"), None),
        P(("groups", "slab"), None),
        P(("groups", "slab"), None),
        P(("groups", "slab")),
        P(None, ("groups", "slab")),
        P(None, None, None, ("groups", "slab")),
        P(None, None, ("groups", "slab")),
    )
    out_specs = (P(None, None, ("groups", "slab")), P("groups", None))
    return jax.shard_map(local, mesh=mesh, in_specs=in_specs, out_specs=out_specs, check_vma=False)
```

```python
import functools
import math

import jax
import jax.numpy as jnp
from jax import lax
from jax.experimental import pallas as pl
from jax.experimental.pallas import tpu as pltpu
from jax.sharding import PartitionSpec as P

VARS = 5
NBR = 6
BY_MATMUL = 3
COMPS = 3
LANES = 128
TILES = 8
GANG = 4
MESH = pl.DeviceIdType.MESH
F32 = jnp.float32
BF16 = jnp.bfloat16


def split_two(value):
    high = value.astype(BF16)
    low = (value - high.astype(F32)).astype(BF16)
    return high, low


def dot_f32(left, right):
    return jnp.dot(left, right, preferred_element_type=F32)


def kernel(
    count, cap, modes, cells,
    shapes_ref, weights_ref, dest_ref, cell_ref, nbr_ref, coupling_ref, inv_ref,
    state_ref, table_ref,
    tail, outgoing, arrived, loads, tag_rows, hot, scaled, start, middle, first, second, gathered,
    edges, halos, part, sums, whole,
    send_a, recv_a, send_h, recv_h, send_g, recv_g, send_w, recv_w, state_sem,
):
    me = lax.axis_index("slab")
    nodes = dest_ref.shape[1]
    groups = LANES // cap
    width = modes // groups
    rows = COMPS * width + 16
    tall = VARS * modes
    span = cells // TILES
    step = count // TILES

    def remote(src, dst, send, recv, peer):
        return pltpu.make_async_remote_copy(
            src_ref=src, dst_ref=dst, send_sem=send, recv_sem=recv,
            device_id={"slab": peer}, device_id_type=MESH,
        )

    barrier = pltpu.get_barrier_semaphore()
    for shift in range(1, count):
        pl.semaphore_signal(
            barrier, inc=1, device_id={"slab": lax.rem(me + shift, count)}, device_id_type=MESH
        )
    halos[...] = jnp.zeros_like(halos)

    dest = dest_ref[...]
    height = -(-count // 16) * 16
    names = dest == lax.broadcasted_iota(jnp.int32, (height, nodes), 0)
    earlier = (
        lax.broadcasted_iota(jnp.int32, (nodes, nodes), 0)
        < lax.broadcasted_iota(jnp.int32, (nodes, nodes), 1)
    )
    before = dot_f32(names.astype(F32).astype(BF16), earlier.astype(F32).astype(BF16))
    rank = jnp.sum(jnp.where(names, before, 0.0), axis=0, keepdims=True)
    place = jnp.broadcast_to(dest.astype(F32) * LANES + rank, (8, nodes)).T[:, 0:1].astype(jnp.int32)
    lane = lax.broadcasted_iota(jnp.int32, (nodes, LANES), 1)
    tail[0 : COMPS * VARS] = weights_ref[...]
    tail[COMPS * VARS : COMPS * VARS + 1] = cell_ref[...].astype(F32)
    pieces = []
    for group in range(groups):
        taken = [
            shapes_ref[comp * modes + group * width : comp * modes + (group + 1) * width]
            for comp in range(COMPS)
        ]
        pieces.append(jnp.concatenate(taken + [tail[...]], axis=0))
    packed = jnp.concatenate(split_two(jnp.concatenate(pieces, axis=1)), axis=0)

    def pack_for(slab):
        at = place - slab * LANES
        picks = jnp.concatenate(
            [(at + group * cap == lane).astype(F32).astype(BF16) for group in range(groups)], axis=0
        )
        both = dot_f32(packed, picks)
        return both[:rows] + both[rows:]

    pl.semaphore_wait(barrier, count - 1)

    def send_step(shift, carry):
        slab = lax.rem(me + shift, count)
        outgoing[slab] = pack_for(slab)
        remote(outgoing.at[slab], arrived.at[me], send_a.at[slab], recv_a.at[me], slab).start()
        return carry

    lax.fori_loop(1, count, send_step, 0)
    arrived[me] = pack_for(me)

    first_cell = me * cells - span
    window = lax.broadcasted_iota(jnp.int32, (3 * span, span), 0)

    def hot_step(block, carry):
        at = pl.ds(pl.multiple_of(block * span, span), span)
        for slot in range(BY_MATMUL):
            names_now = nbr_ref[slot : slot + 1, at]
            local = jnp.where(names_now >= 0, names_now - (first_cell + block * span), -1)
            hot[block, :, slot * span : (slot + 1) * span] = (window == local).astype(F32).astype(BF16)
        return carry

    lax.fori_loop(0, TILES, hot_step, 0)

    filled = nbr_ref[...] >= 0
    for in_var in range(VARS):
        def scale_step(out_var, carry):
            total = inv_ref[out_var, 0:1, :] * coupling_ref[0, in_var]
            for mid in range(1, VARS):
                total = total + inv_ref[out_var, mid : mid + 1, :] * coupling_ref[mid, in_var]
            scaled[out_var, in_var] = jnp.where(filled, total, 0.0)
            return carry

        lax.fori_loop(0, VARS, scale_step, 0)

    def arrive_step(shift, carry):
        slab = lax.rem(me + shift, count)
        remote(outgoing.at[slab], arrived.at[slab], send_a.at[slab], recv_a.at[slab], slab).wait()
        return carry

    lax.fori_loop(1, count, arrive_step, 0)

    part_of = lax.broadcasted_iota(jnp.int32, (1, LANES), 1) // cap

    def load_step(bunch, carry):
        at = pl.ds(pl.multiple_of(bunch * LANES, LANES), LANES)
        tags = jnp.zeros((1, LANES), F32)
        built = [[None] * groups for _ in range(VARS)]
        for turn in range(groups):
            here = part_of == turn
            data = arrived[bunch * groups + turn]
            base = COMPS * width
            tags = jnp.where(here, data[base + 15 : base + 16], tags)
            for var in range(VARS):
                load = data[base + COMPS * var : base + COMPS * var + 1] * data[:width]
                for comp in range(1, COMPS):
                    at_row = base + COMPS * var + comp
                    load = load + data[at_row : at_row + 1] * data[comp * width : (comp + 1) * width]
                for group in range(groups):
                    turn_by = ((turn - group) * cap) % LANES
                    moved = pltpu.roll(load, turn_by, 1) if turn_by else load
                    kept = built[var][group]
                    built[var][group] = moved if kept is None else jnp.where(here, moved, kept)
        for var in range(VARS):
            high, low = split_two(jnp.concatenate(built[var], axis=0))
            loads[var * modes : (var + 1) * modes, at] = high
            loads[tall + var * modes : tall + (var + 1) * modes, at] = low
        tag_rows[:, at] = jnp.broadcast_to(tags, (8, LANES))
        return carry

    lax.fori_loop(0, count // groups, load_step, 0)
    tag_column = tag_rows[...].T[:, 0:1].astype(jnp.int32)
    slot_cells = lax.broadcasted_iota(jnp.int32, (count * cap, span), 1)

    def keep(state, block, var, value):
        high, low = split_two(value)
        state[block + 1, var * modes : (var + 1) * modes] = high
        state[block + 1, tall + var * modes : tall + (var + 1) * modes] = low

    def begin(block, side):
        at = pl.ds(pl.multiple_of(block * span, span), span)
        matches = (tag_column == slot_cells + block * span).astype(F32).astype(BF16)
        both = dot_f32(loads[...], matches)
        forcing = both[:tall] + both[tall:]
        for var in range(VARS):
            total = inv_ref[var, 0:1, at] * forcing[:modes]
            for mid in range(1, VARS):
                total = total + inv_ref[var, mid : mid + 1, at] * forcing[mid * modes : (mid + 1) * modes]
            start[block + 1, var * modes : (var + 1) * modes] = total
            keep(first, block, var, total)
            if side is not None:
                edges[0, side, var * modes : (var + 1) * modes] = total

    def sweep(source, wide, target, kept, block, side):
        at = pl.ds(pl.multiple_of(block * span, span), span)
        near = jnp.concatenate([source[block], source[block + 1], source[block + 2]], axis=1)
        for slot in range(BY_MATMUL):
            both = dot_f32(near, hot[block, :, slot * span : (slot + 1) * span])
            gathered[slot] = both[:tall] + both[tall:]
        for half in range(span // LANES):
            for slot in range(BY_MATMUL, NBR):
                here = pl.ds(pl.multiple_of(block * span + half * LANES, LANES), LANES)
                local = nbr_ref[slot : slot + 1, here] - (first_cell + block * span + half * LANES)
                lanes = jnp.broadcast_to(jnp.bitwise_and(local, LANES - 1), (modes, LANES))
                tile = jnp.broadcast_to(lax.shift_right_arithmetic(local, 7), (modes, LANES))
                for var in range(VARS):
                    picked = None
                    for index in range(2 * span // LANES + 1):
                        at_block, at_half = divmod(half + index, span // LANES)
                        values = wide[
                            block + at_block, var * modes : (var + 1) * modes,
                            at_half * LANES : (at_half + 1) * LANES,
                        ]
                        taken = jnp.take_along_axis(values, lanes, axis=1, mode="promise_in_bounds")
                        picked = taken if picked is None else jnp.where(tile == index, taken, picked)
                    gathered[slot, var * modes : (var + 1) * modes, half * LANES : (half + 1) * LANES] = picked
        for var in range(VARS):
            total = start[block + 1, var * modes : (var + 1) * modes]
            for slot in range(NBR):
                for mid in range(VARS):
                    total = total - (
                        scaled[var, mid, slot : slot + 1, at]
                        * gathered[slot, mid * modes : (mid + 1) * modes]
                    )
            keep(target, block, var, total)
            if kept is not None:
                kept[block + 1, var * modes : (var + 1) * modes] = total
            if side is not None:
                edges[1, side, var * modes : (var + 1) * modes] = total

    def halo_copy(turn, side):
        peer = me - 1 if side == 0 else me + 1
        return remote(
            edges.at[turn, side], halos.at[turn, 1 - side],
            send_h.at[turn, side], recv_h.at[turn, 1 - side], peer,
        )

    def halo_wait(turn, side):
        peer = me - 1 if side == 0 else me + 1
        return remote(
            edges.at[turn, side], halos.at[turn, side],
            send_h.at[turn, side], recv_h.at[turn, side], peer,
        )

    def halo_send(turn):
        @pl.when(me > 0)
        def _():
            halo_copy(turn, 0).start()

        @pl.when(me < count - 1)
        def _():
            halo_copy(turn, 1).start()

    def halo_take(turn, state, wide):
        @pl.when(me > 0)
        def _():
            halo_wait(turn, 0).wait()

        @pl.when(me < count - 1)
        def _():
            halo_wait(turn, 1).wait()

        for side, block in ((0, -1), (1, TILES)):
            for var in range(VARS):
                value = halos[turn, side, var * modes : (var + 1) * modes]
                keep(state, block, var, value)
                wide[block + 1, var * modes : (var + 1) * modes] = value

    last = TILES - 1
    begin(0, 0)
    begin(last, 1)
    halo_send(0)

    def begin_step(block, carry):
        begin(block, None)
        return carry

    lax.fori_loop(1, last, begin_step, 0)

    def first_step(block, carry):
        sweep(first, start, second, middle, block, None)
        return carry

    def second_step(block, carry):
        sweep(second, middle, first, None, block, None)
        return carry

    lax.fori_loop(1, TILES // 2, first_step, 0)
    halo_take(0, first, start)
    sweep(first, start, second, middle, 0, 0)
    sweep(first, start, second, middle, last, 1)
    halo_send(1)
    lax.fori_loop(TILES // 2, last, first_step, 0)
    lax.fori_loop(1, last, second_step, 0)
    halo_take(1, second, middle)
    sweep(second, middle, first, None, 0, None)
    sweep(second, middle, first, None, last, None)

    state_copy = pltpu.make_async_copy(first.at[pl.ds(1, TILES)], state_ref, state_sem)
    state_copy.start()

    def gram_step(block, total):
        for var in range(VARS):
            stack = jnp.concatenate(
                [
                    first[block + 1, var * modes : (var + 1) * modes],
                    first[block + 1, tall + var * modes : tall + (var + 1) * modes],
                ],
                axis=0,
            )
            total = total + lax.dot_general(
                stack, stack, (((1,), (1,)), ((), ())), preferred_element_type=F32
            )
        return total

    gram = lax.fori_loop(0, TILES, gram_step, jnp.zeros((2 * modes, 2 * modes), F32))
    gram = gram[:modes] + gram[modes:]
    gram = gram + pltpu.roll(gram, modes, 1)
    high = modes // TILES
    for tile in range(TILES):
        owner = tile * step
        part[tile] = gram[tile * high : (tile + 1) * high]

        @pl.when(me != owner)
        def _():
            remote(part.at[tile], sums.at[me], send_g.at[tile], recv_g.at[me], owner).start()

        @pl.when(me == owner)
        def _():
            sums[me] = part[tile]

    mine = me // step

    @pl.when(lax.rem(me, step) == 0)
    def _():
        def sum_wait(shift, carry):
            slab = lax.rem(me + shift, count)
            remote(part.at[0], sums.at[slab], send_g.at[0], recv_g.at[slab], slab).wait_recv()
            return carry

        lax.fori_loop(1, count, sum_wait, 0)
        total = sums[0]
        for slab in range(1, count):
            total = total + sums[slab]
        whole[mine] = total
        for shift in range(1, count):
            slab = lax.rem(me + shift, count)
            remote(whole.at[mine], whole.at[mine], send_w.at[slab], recv_w.at[mine], slab).start()

    for tile in range(TILES):
        owner = tile * step

        @pl.when(me != owner)
        def _():
            remote(part.at[tile], sums.at[me], send_g.at[tile], recv_g.at[me], owner).wait_send()
            remote(whole.at[tile], whole.at[tile], send_w.at[0], recv_w.at[tile], owner).wait_recv()

    table_ref[...] = jnp.concatenate([whole[tile] for tile in range(TILES)], axis=0)
    state_copy.wait()

    @pl.when(lax.rem(me, step) == 0)
    def _():
        for shift in range(1, count):
            slab = lax.rem(me + shift, count)
            remote(whole.at[mine], whole.at[mine], send_w.at[slab], recv_w.at[mine], slab).wait_send()


def finish(modes, scale, table_ref, state_ref, basis_ref, factor_ref, mixer):
    high = modes // TILES
    tall = VARS * modes

    @pl.when(pl.program_id(0) == 0)
    def _():
        row_at = lax.broadcasted_iota(jnp.int32, (modes, 2 * modes), 0)
        col_at = lax.broadcasted_iota(jnp.int32, (modes, 2 * modes), 1)
        table = table_ref[...]
        table = jnp.where(col_at < modes, table, jnp.where(col_at - modes == row_at, 1.0, 0.0))
        bands = [table[tile * high : (tile + 1) * high] for tile in range(TILES)]
        inner = lax.broadcasted_iota(jnp.int32, (high, 2 * modes), 0)
        for pivot_at in range(0, modes, GANG):
            band, offset = pivot_at // high, pivot_at % high
            columns = [
                {
                    tile: jnp.broadcast_to(bands[tile][:, pivot_at + q : pivot_at + q + 1], (high, 2 * modes))
                    for tile in range(band, TILES)
                }
                for q in range(GANG)
            ]
            rows = [bands[band][offset + q : offset + q + 1] for q in range(GANG)]
            for q in range(GANG):
                marks = [columns[q][band][offset + r : offset + r + 1] for r in range(GANG)]
                inverse = 1.0 / marks[q]
                row = rows[q] * inverse
                for r in range(q + 1, GANG):
                    ratio = marks[r] * inverse
                    for tile in range(band, TILES):
                        columns[r][tile] = columns[r][tile] - columns[q][tile] * ratio
                    rows[r] = rows[r] - marks[r] * row
                for tile in range(band, TILES):
                    column = columns[q][tile]
                    if tile == band:
                        column = jnp.where(inner > offset + q, column, 0.0)
                    bands[tile] = bands[tile] - column * row
        table = jnp.concatenate(bands, axis=0)
        diagonal = jnp.sum(jnp.where(col_at == row_at, table, 0.0), axis=1, keepdims=True)
        root = jnp.sqrt(diagonal)
        upper = jnp.where(col_at >= row_at, table * (root / diagonal) * (1.0 / scale), 0.0)
        factor_ref[...] = upper[:, :modes]
        inverse = pltpu.roll(table * (scale / root), modes, 1)[:, :modes]
        inv_high, inv_low = split_two(inverse)
        mixer[...] = jnp.concatenate([inv_high, inv_high, inv_low], axis=1)

    for var in range(VARS):
        top = state_ref[0, var * modes : (var + 1) * modes]
        bottom = state_ref[0, tall + var * modes : tall + (var + 1) * modes]
        basis_ref[var] = dot_f32(mixer[...], jnp.concatenate([top, bottom, top], axis=0))


def local(
    mode_shapes, wall_coupling, owner_dev, owner_cell, neighbours, coupling_blocks, inv_blocks
):
    count = lax.axis_size("slab")
    cells = inv_blocks.shape[2]
    nodes = mode_shapes.shape[0]
    modes = mode_shapes.shape[1] // COMPS
    cap = max(2, 2 * nodes // count)
    groups = LANES // cap
    rows = COMPS * (modes // groups) + 16
    tall = VARS * modes
    span = cells // TILES
    scale = math.sqrt(VARS * cells * count)
    vmem = pl.BlockSpec(memory_space=pltpu.VMEM)
    dma = pltpu.SemaphoreType.DMA
    state, table = pl.pallas_call(
        functools.partial(kernel, count, cap, modes, cells),
        out_shape=(
            jax.ShapeDtypeStruct((TILES, 2 * tall, span), BF16),
            jax.ShapeDtypeStruct((modes, 2 * modes), F32),
        ),
        in_specs=[vmem] * 7,
        out_specs=(pl.BlockSpec(memory_space=pl.ANY), vmem),
        scratch_shapes=[
            pltpu.VMEM((16, nodes), F32),
            pltpu.VMEM((count, rows, LANES), F32),
            pltpu.VMEM((count, rows, LANES), F32),
            pltpu.VMEM((2 * tall, count * cap), BF16),
            pltpu.VMEM((8, count * cap), F32),
            pltpu.VMEM((TILES, 3 * span, max(1, BY_MATMUL) * span), BF16),
            pltpu.VMEM((VARS, VARS, NBR, cells), F32),
            pltpu.VMEM((TILES + 2, tall, span), F32),
            pltpu.VMEM((TILES + 2, tall, span), F32),
            pltpu.VMEM((TILES + 2, 2 * tall, span), BF16),
            pltpu.VMEM((TILES + 2, 2 * tall, span), BF16),
            pltpu.VMEM((NBR, tall, span), F32),
            pltpu.VMEM((2, 2, tall, span), F32),
            pltpu.VMEM((2, 2, tall, span), F32),
            pltpu.VMEM((TILES, modes // TILES, 2 * modes), F32),
            pltpu.VMEM((count, modes // TILES, 2 * modes), F32),
            pltpu.VMEM((TILES, modes // TILES, 2 * modes), F32),
            dma((count,)), dma((count,)), dma((2, 2)), dma((2, 2)),
            dma((TILES,)), dma((count,)), dma((count,)), dma((TILES,)), dma,
        ],
        compiler_params=pltpu.CompilerParams(
            collective_id=0, has_side_effects=True, vmem_limit_bytes=58 * 1024 * 1024
        ),
    )(
        mode_shapes.T, wall_coupling.T, owner_dev.T, owner_cell.reshape(1, nodes), neighbours,
        coupling_blocks.transpose(1, 2, 0, 3), inv_blocks,
    )
    return pl.pallas_call(
        functools.partial(finish, modes, scale),
        grid=(TILES,),
        out_shape=(
            jax.ShapeDtypeStruct((VARS, modes, cells), F32),
            jax.ShapeDtypeStruct((modes, modes), F32),
        ),
        in_specs=[
            pl.BlockSpec((modes, 2 * modes), lambda block: (0, 0)),
            pl.BlockSpec((1, 2 * tall, span), lambda block: (block, 0, 0)),
        ],
        out_specs=(
            pl.BlockSpec((VARS, modes, span), lambda block: (0, 0, block)),
            pl.BlockSpec((modes, modes), lambda block: (0, 0)),
        ),
        scratch_shapes=[pltpu.VMEM((modes, 3 * modes), BF16)],
    )(table, state)


def solution(mesh):
    in_specs = (
        P(("groups", "slab"), None),
        P(("groups", "slab"), None),
        P(("groups", "slab"), None),
        P(("groups", "slab")),
        P(None, ("groups", "slab")),
        P(None, None, None, ("groups", "slab")),
        P(None, None, ("groups", "slab")),
    )
    out_specs = (P(None, None, ("groups", "slab")), P("groups", None))
    return jax.shard_map(local, mesh=mesh, in_specs=in_specs, out_specs=out_specs, check_vma=False)
```

```python
import functools
import math

import jax
import jax.numpy as jnp
from jax import lax
from jax.experimental import pallas as pl
from jax.experimental.pallas import tpu as pltpu
from jax.sharding import PartitionSpec as P

VARS = 5
NBR = 6
BY_MATMUL = 3
COMPS = 3
LANES = 128
TILES = 8
GANG = 8
MESH = pl.DeviceIdType.MESH
F32 = jnp.float32
BF16 = jnp.bfloat16


def split_two(value):
    high = value.astype(BF16)
    low = (value - high.astype(F32)).astype(BF16)
    return high, low


def dot_f32(left, right):
    return jnp.dot(left, right, preferred_element_type=F32)


def kernel(
    count, cap, modes, cells,
    shapes_ref, weights_ref, dest_ref, cell_ref, nbr_ref, coupling_ref, inv_ref,
    state_ref, table_ref,
    tail, outgoing, arrived, loads, tag_rows, hot, scaled, start, middle, first, second, even, odd,
    part, sums, whole,
    send_a, recv_a, send_h, recv_h, send_g, recv_g, send_w, recv_w, state_sem,
):
    me = lax.axis_index("slab")
    nodes = dest_ref.shape[1]
    groups = LANES // cap
    width = modes // groups
    rows = COMPS * width + 16
    tall = VARS * modes
    span = cells // TILES
    step = count // TILES

    def remote(src, dst, send, recv, peer):
        return pltpu.make_async_remote_copy(
            src_ref=src, dst_ref=dst, send_sem=send, recv_sem=recv,
            device_id={"slab": peer}, device_id_type=MESH,
        )

    barrier = pltpu.get_barrier_semaphore()
    for shift in range(1, count):
        pl.semaphore_signal(
            barrier, inc=1, device_id={"slab": lax.rem(me + shift, count)}, device_id_type=MESH
        )
    for wide in (start, middle):
        wide[0] = jnp.zeros_like(wide[0])
        wide[TILES + 1] = jnp.zeros_like(wide[0])

    dest = dest_ref[...]
    height = -(-count // 16) * 16
    names = dest == lax.broadcasted_iota(jnp.int32, (height, nodes), 0)
    earlier = (
        lax.broadcasted_iota(jnp.int32, (nodes, nodes), 0)
        < lax.broadcasted_iota(jnp.int32, (nodes, nodes), 1)
    )
    before = dot_f32(names.astype(F32).astype(BF16), earlier.astype(F32).astype(BF16))
    rank = jnp.sum(jnp.where(names, before, 0.0), axis=0, keepdims=True)
    place = jnp.broadcast_to(dest.astype(F32) * LANES + rank, (8, nodes)).T[:, 0:1].astype(jnp.int32)
    lane = lax.broadcasted_iota(jnp.int32, (nodes, LANES), 1)
    tail[0 : COMPS * VARS] = weights_ref[...]
    tail[COMPS * VARS : COMPS * VARS + 1] = cell_ref[...].astype(F32)
    pieces = []
    for group in range(groups):
        taken = [
            shapes_ref[comp * modes + group * width : comp * modes + (group + 1) * width]
            for comp in range(COMPS)
        ]
        pieces.append(jnp.concatenate(taken + [tail[...]], axis=0))
    packed = jnp.concatenate(split_two(jnp.concatenate(pieces, axis=1)), axis=0)

    def pack_for(slab):
        at = place - slab * LANES
        picks = jnp.concatenate(
            [(at + group * cap == lane).astype(F32).astype(BF16) for group in range(groups)], axis=0
        )
        both = dot_f32(packed, picks)
        return both[:rows] + both[rows:]

    pl.semaphore_wait(barrier, count - 1)

    def send_step(shift, carry):
        slab = lax.rem(me + shift, count)
        outgoing[slab] = pack_for(slab)
        remote(outgoing.at[slab], arrived.at[me], send_a.at[slab], recv_a.at[me], slab).start()
        return carry

    lax.fori_loop(1, count, send_step, 0)
    arrived[me] = pack_for(me)

    first_cell = me * cells - span
    window = lax.broadcasted_iota(jnp.int32, (3 * span, span), 0)

    def hot_step(block, carry):
        at = pl.ds(pl.multiple_of(block * span, span), span)
        for slot in range(BY_MATMUL):
            names_now = nbr_ref[slot : slot + 1, at]
            local = jnp.where(names_now >= 0, names_now - (first_cell + block * span), -1)
            hot[block, :, slot * span : (slot + 1) * span] = (window == local).astype(F32).astype(BF16)
        return carry

    lax.fori_loop(0, TILES, hot_step, 0)

    filled = nbr_ref[...] >= 0
    for in_var in range(VARS):
        def scale_step(out_var, carry):
            total = inv_ref[out_var, 0:1, :] * coupling_ref[0, in_var]
            for mid in range(1, VARS):
                total = total + inv_ref[out_var, mid : mid + 1, :] * coupling_ref[mid, in_var]
            scaled[out_var, in_var] = jnp.where(filled, total, 0.0)
            return carry

        lax.fori_loop(0, VARS, scale_step, 0)

    part_of = lax.broadcasted_iota(jnp.int32, (1, LANES), 1) // cap
    depth = loads.shape[1]
    per_chunk = depth // cap
    chunks = count // per_chunk

    def take_chunk(chunk):
        for turn in range(per_chunk):
            shift = chunk * per_chunk + turn
            slab = lax.rem(me - shift + count, count)

            @pl.when(shift > 0)
            def _():
                remote(outgoing.at[slab], arrived.at[slab], send_a.at[slab], recv_a.at[slab], slab).wait_recv()

        for bunch in range(depth // LANES):
            tags = jnp.zeros((1, LANES), F32)
            built = [[None] * groups for _ in range(VARS)]
            for turn in range(groups):
                here = part_of == turn
                shift = chunk * per_chunk + bunch * groups + turn
                data = arrived[lax.rem(me - shift + count, count)]
                base = COMPS * width
                tags = jnp.where(here, data[base + 15 : base + 16], tags)
                for var in range(VARS):
                    load = data[base + COMPS * var : base + COMPS * var + 1] * data[:width]
                    for comp in range(1, COMPS):
                        at_row = base + COMPS * var + comp
                        load = load + data[at_row : at_row + 1] * data[comp * width : (comp + 1) * width]
                    for group in range(groups):
                        turn_by = ((turn - group) * cap) % LANES
                        moved = pltpu.roll(load, turn_by, 1) if turn_by else load
                        kept = built[var][group]
                        built[var][group] = moved if kept is None else jnp.where(here, moved, kept)
            at = slice(bunch * LANES, (bunch + 1) * LANES)
            for var in range(VARS):
                high, low = split_two(jnp.concatenate(built[var], axis=0))
                loads[var * modes : (var + 1) * modes, at] = high
                loads[tall + var * modes : tall + (var + 1) * modes, at] = low
            tag_rows[:, at] = jnp.broadcast_to(tags, (8, LANES))
        return tag_rows[...].T[:, 0:1].astype(jnp.int32)

    slot_cells = lax.broadcasted_iota(jnp.int32, (depth, span), 1)

    def chunk_forcing(tag_column, block):
        matches = (tag_column == slot_cells + block * span).astype(F32).astype(BF16)
        both = dot_f32(loads[...], matches)
        return both[:tall] + both[tall:]

    tag_first = take_chunk(0)

    def open_step(block, carry):
        start[block + 1] = chunk_forcing(tag_first, block)
        return carry

    lax.fori_loop(0, TILES, open_step, 0)

    def chunk_step(chunk, carry):
        tag_column = take_chunk(chunk)

        def add_step(block, carry):
            start[block + 1] = start[block + 1] + chunk_forcing(tag_column, block)
            return carry

        return lax.fori_loop(0, TILES, add_step, carry)

    lax.fori_loop(1, chunks - 1, chunk_step, 0)
    tag_last = take_chunk(chunks - 1)

    def keep(state, block, var, value):
        high, low = split_two(value)
        state[block + 1, var * modes : (var + 1) * modes] = high
        state[block + 1, tall + var * modes : tall + (var + 1) * modes] = low

    def halo(wide, turn, side):
        peer = me - 1 if side == 0 else me + 1
        near, far = (1, TILES + 1) if side == 0 else (TILES, 0)
        return remote(
            wide.at[near], wide.at[far], send_h.at[turn, side], recv_h.at[turn, 1 - side], peer
        )

    def halo_arrival(wide, turn, side):
        peer = me - 1 if side == 0 else me + 1
        near, far = (1, 0) if side == 0 else (TILES, TILES + 1)
        return remote(wide.at[near], wide.at[far], send_h.at[turn, side], recv_h.at[turn, side], peer)

    def halo_send(wide, turn):
        @pl.when(me > 0)
        def _():
            halo(wide, turn, 0).start()

        @pl.when(me < count - 1)
        def _():
            halo(wide, turn, 1).start()

    def halo_take(wide, turn, state):
        @pl.when(me > 0)
        def _():
            halo_arrival(wide, turn, 0).wait()

        @pl.when(me < count - 1)
        def _():
            halo_arrival(wide, turn, 1).wait()

        for block in (-1, TILES):
            for var in range(VARS):
                keep(state, block, var, wide[block + 1, var * modes : (var + 1) * modes])

    def begin_step(turn, carry):
        block = lax.rem(turn * (TILES - 1), TILES)
        at = pl.ds(pl.multiple_of(block * span, span), span)
        forcing = start[block + 1] + chunk_forcing(tag_last, block)
        for var in range(VARS):
            total = inv_ref[var, 0:1, at] * forcing[:modes]
            for mid in range(1, VARS):
                total = total + inv_ref[var, mid : mid + 1, at] * forcing[mid * modes : (mid + 1) * modes]
            start[block + 1, var * modes : (var + 1) * modes] = total
            keep(first, block, var, total)
        return carry

    lax.fori_loop(0, 2, begin_step, 0)
    halo_send(start, 0)
    lax.fori_loop(2, TILES, begin_step, 0)

    def gather(source, wide, gathered, block):
        near = jnp.concatenate([source[block], source[block + 1], source[block + 2]], axis=1)
        for slot in range(BY_MATMUL):
            both = dot_f32(near, hot[block, :, slot * span : (slot + 1) * span])
            gathered[slot] = both[:tall] + both[tall:]
        for half in range(span // LANES):
            for slot in range(BY_MATMUL, NBR):
                here = pl.ds(pl.multiple_of(block * span + half * LANES, LANES), LANES)
                local = nbr_ref[slot : slot + 1, here] - (first_cell + block * span + half * LANES)
                lanes = jnp.broadcast_to(jnp.bitwise_and(local, LANES - 1), (modes, LANES))
                tile = jnp.broadcast_to(lax.shift_right_arithmetic(local, 7), (modes, LANES))
                for var in range(VARS):
                    picked = None
                    for index in range(2 * span // LANES + 1):
                        at_block, at_half = divmod(half + index, span // LANES)
                        values = wide[
                            block + at_block, var * modes : (var + 1) * modes,
                            at_half * LANES : (at_half + 1) * LANES,
                        ]
                        taken = jnp.take_along_axis(values, lanes, axis=1, mode="promise_in_bounds")
                        picked = taken if picked is None else jnp.where(tile == index, taken, picked)
                    gathered[slot, var * modes : (var + 1) * modes, half * LANES : (half + 1) * LANES] = picked

    def mix(gathered, target, kept, block):
        at = pl.ds(pl.multiple_of(block * span, span), span)
        for var in range(VARS):
            total = start[block + 1, var * modes : (var + 1) * modes]
            for slot in range(NBR):
                for mid in range(VARS):
                    total = total - (
                        scaled[var, mid, slot : slot + 1, at]
                        * gathered[slot, mid * modes : (mid + 1) * modes]
                    )
            keep(target, block, var, total)
            if kept is not None:
                kept[block + 1, var * modes : (var + 1) * modes] = total

    def sweep(source, wide, target, kept, turn):
        def block_of(item):
            return lax.rem(item + 1, TILES)

        gather(source, wide, even, block_of(0))

        def pair_step(pair, carry):
            @pl.when(pair == TILES // 2 - 2)
            def _():
                halo_take(wide, turn, source)

            item = 2 * pair
            gather(source, wide, odd, block_of(item + 1))
            mix(even, target, kept, block_of(item))
            gather(source, wide, even, block_of(item + 2))
            mix(odd, target, kept, block_of(item + 1))
            return carry

        lax.fori_loop(0, TILES // 2 - 1, pair_step, 0)
        gather(source, wide, odd, 0)
        mix(even, target, kept, TILES - 1)
        mix(odd, target, kept, 0)

    sweep(first, start, second, middle, 0)
    halo_send(middle, 1)
    sweep(second, middle, first, None, 1)
    state_copy = pltpu.make_async_copy(first.at[pl.ds(1, TILES)], state_ref, state_sem)
    state_copy.start()

    def gram_step(block, total):
        for var in range(VARS):
            stack = jnp.concatenate(
                [
                    first[block + 1, var * modes : (var + 1) * modes],
                    first[block + 1, tall + var * modes : tall + (var + 1) * modes],
                ],
                axis=0,
            )
            total = total + lax.dot_general(
                stack, stack, (((1,), (1,)), ((), ())), preferred_element_type=F32
            )
        return total

    gram = lax.fori_loop(0, TILES, gram_step, jnp.zeros((2 * modes, 2 * modes), F32))
    gram = gram[:modes] + gram[modes:]
    gram = gram + pltpu.roll(gram, modes, 1)
    high = modes // TILES
    for tile in range(TILES):
        owner = tile * step
        part[tile] = gram[tile * high : (tile + 1) * high]

        @pl.when(me != owner)
        def _():
            remote(part.at[tile], sums.at[me], send_g.at[tile], recv_g.at[me], owner).start()

        @pl.when(me == owner)
        def _():
            sums[me] = part[tile]

    mine = me // step

    @pl.when(lax.rem(me, step) == 0)
    def _():
        def sum_wait(shift, carry):
            slab = lax.rem(me + shift, count)
            remote(part.at[0], sums.at[slab], send_g.at[0], recv_g.at[slab], slab).wait_recv()
            return carry

        lax.fori_loop(1, count, sum_wait, 0)
        total = sums[0]
        for slab in range(1, count):
            total = total + sums[slab]
        whole[mine] = total
        for shift in range(1, count):
            slab = lax.rem(me + shift, count)
            remote(whole.at[mine], whole.at[mine], send_w.at[slab], recv_w.at[mine], slab).start()

    for tile in range(TILES):
        owner = tile * step

        @pl.when(me != owner)
        def _():
            remote(part.at[tile], sums.at[me], send_g.at[tile], recv_g.at[me], owner).wait_send()
            remote(whole.at[tile], whole.at[tile], send_w.at[0], recv_w.at[tile], owner).wait_recv()

    def sent_step(shift, carry):
        slab = lax.rem(me + shift, count)
        remote(outgoing.at[slab], arrived.at[me], send_a.at[slab], recv_a.at[me], slab).wait_send()
        return carry

    lax.fori_loop(1, count, sent_step, 0)
    table_ref[...] = jnp.concatenate([whole[tile] for tile in range(TILES)], axis=0)
    state_copy.wait()

    @pl.when(lax.rem(me, step) == 0)
    def _():
        for shift in range(1, count):
            slab = lax.rem(me + shift, count)
            remote(whole.at[mine], whole.at[mine], send_w.at[slab], recv_w.at[mine], slab).wait_send()


def finish(modes, scale, table_ref, state_ref, basis_ref, factor_ref, mixer):
    high = modes // TILES
    tall = VARS * modes

    @pl.when(pl.program_id(0) == 0)
    def _():
        row_at = lax.broadcasted_iota(jnp.int32, (modes, 2 * modes), 0)
        col_at = lax.broadcasted_iota(jnp.int32, (modes, 2 * modes), 1)
        table = table_ref[...]
        table = jnp.where(col_at < modes, table, jnp.where(col_at - modes == row_at, 1.0, 0.0))
        bands = [table[tile * high : (tile + 1) * high] for tile in range(TILES)]
        inner = lax.broadcasted_iota(jnp.int32, (high, 2 * modes), 0)
        for pivot_at in range(0, modes, GANG):
            band, offset = pivot_at // high, pivot_at % high
            columns = [
                {
                    tile: jnp.broadcast_to(bands[tile][:, pivot_at + q : pivot_at + q + 1], (high, 2 * modes))
                    for tile in range(band, TILES)
                }
                for q in range(GANG)
            ]
            rows = [bands[band][offset + q : offset + q + 1] for q in range(GANG)]
            for q in range(GANG):
                marks = [columns[q][band][offset + r : offset + r + 1] for r in range(GANG)]
                inverse = 1.0 / marks[q]
                row = rows[q] * inverse
                for r in range(q + 1, GANG):
                    ratio = marks[r] * inverse
                    for tile in range(band, TILES):
                        columns[r][tile] = columns[r][tile] - columns[q][tile] * ratio
                    rows[r] = rows[r] - marks[r] * row
                for tile in range(band, TILES):
                    column = columns[q][tile]
                    if tile == band:
                        column = jnp.where(inner > offset + q, column, 0.0)
                    bands[tile] = bands[tile] - column * row
        table = jnp.concatenate(bands, axis=0)
        diagonal = jnp.sum(jnp.where(col_at == row_at, table, 0.0), axis=1, keepdims=True)
        root = jnp.sqrt(diagonal)
        upper = jnp.where(col_at >= row_at, table * (root / diagonal) * (1.0 / scale), 0.0)
        factor_ref[...] = upper[:, :modes]
        inverse = pltpu.roll(table * (scale / root), modes, 1)[:, :modes]
        inv_high, inv_low = split_two(inverse)
        mixer[...] = jnp.concatenate([inv_high, inv_high, inv_low], axis=1)

    for var in range(VARS):
        top = state_ref[0, var * modes : (var + 1) * modes]
        bottom = state_ref[0, tall + var * modes : tall + (var + 1) * modes]
        basis_ref[var] = dot_f32(mixer[...], jnp.concatenate([top, bottom, top], axis=0))


def local(
    mode_shapes, wall_coupling, owner_dev, owner_cell, neighbours, coupling_blocks, inv_blocks
):
    count = lax.axis_size("slab")
    cells = inv_blocks.shape[2]
    nodes = mode_shapes.shape[0]
    modes = mode_shapes.shape[1] // COMPS
    cap = max(2, 2 * nodes // count)
    groups = LANES // cap
    rows = COMPS * (modes // groups) + 16
    tall = VARS * modes
    span = cells // TILES
    scale = math.sqrt(VARS * cells * count)
    vmem = pl.BlockSpec(memory_space=pltpu.VMEM)
    dma = pltpu.SemaphoreType.DMA
    state, table = pl.pallas_call(
        functools.partial(kernel, count, cap, modes, cells),
        out_shape=(
            jax.ShapeDtypeStruct((TILES, 2 * tall, span), BF16),
            jax.ShapeDtypeStruct((modes, 2 * modes), F32),
        ),
        in_specs=[vmem] * 7,
        out_specs=(pl.BlockSpec(memory_space=pl.ANY), vmem),
        scratch_shapes=[
            pltpu.VMEM((16, nodes), F32),
            pltpu.VMEM((count, rows, LANES), F32),
            pltpu.VMEM((count, rows, LANES), F32),
            pltpu.VMEM((2 * tall, 2 * LANES), BF16),
            pltpu.VMEM((8, 2 * LANES), F32),
            pltpu.VMEM((TILES, 3 * span, max(1, BY_MATMUL) * span), BF16),
            pltpu.VMEM((VARS, VARS, NBR, cells), F32),
            pltpu.VMEM((TILES + 2, tall, span), F32),
            pltpu.VMEM((TILES + 2, tall, span), F32),
            pltpu.VMEM((TILES + 2, 2 * tall, span), BF16),
            pltpu.VMEM((TILES + 2, 2 * tall, span), BF16),
            pltpu.VMEM((NBR, tall, span), F32),
            pltpu.VMEM((NBR, tall, span), F32),
            pltpu.VMEM((TILES, modes // TILES, 2 * modes), F32),
            pltpu.VMEM((count, modes // TILES, 2 * modes), F32),
            pltpu.VMEM((TILES, modes // TILES, 2 * modes), F32),
            dma((count,)), dma((count,)), dma((2, 2)), dma((2, 2)),
            dma((TILES,)), dma((count,)), dma((count,)), dma((TILES,)), dma,
        ],
        compiler_params=pltpu.CompilerParams(
            collective_id=0, has_side_effects=True, vmem_limit_bytes=58 * 1024 * 1024
        ),
    )(
        mode_shapes.T, wall_coupling.T, owner_dev.T, owner_cell.reshape(1, nodes), neighbours,
        coupling_blocks.transpose(1, 2, 0, 3), inv_blocks,
    )
    return pl.pallas_call(
        functools.partial(finish, modes, scale),
        grid=(TILES,),
        out_shape=(
            jax.ShapeDtypeStruct((VARS, modes, cells), F32),
            jax.ShapeDtypeStruct((modes, modes), F32),
        ),
        in_specs=[
            pl.BlockSpec((modes, 2 * modes), lambda block: (0, 0)),
            pl.BlockSpec((1, 2 * tall, span), lambda block: (block, 0, 0)),
        ],
        out_specs=(
            pl.BlockSpec((VARS, modes, span), lambda block: (0, 0, block)),
            pl.BlockSpec((modes, modes), lambda block: (0, 0)),
        ),
        scratch_shapes=[pltpu.VMEM((modes, 3 * modes), BF16)],
    )(table, state)


def solution(mesh):
    in_specs = (
        P(("groups", "slab"), None),
        P(("groups", "slab"), None),
        P(("groups", "slab"), None),
        P(("groups", "slab")),
        P(None, ("groups", "slab")),
        P(None, None, None, ("groups", "slab")),
        P(None, None, ("groups", "slab")),
    )
    out_specs = (P(None, None, ("groups", "slab")), P("groups", None))
    return jax.shard_map(local, mesh=mesh, in_specs=in_specs, out_specs=out_specs, check_vma=False)
```

```python
import functools
import math

import jax
import jax.numpy as jnp
from jax import lax
from jax.experimental import pallas as pl
from jax.experimental.pallas import tpu as pltpu
from jax.sharding import PartitionSpec as P

VARS = 5
NBR = 6
COMPS = 3
LANES = 128
TILES = 8
BAND = 32
GANG = 8
MESH = pl.DeviceIdType.MESH
F32 = jnp.float32
BF16 = jnp.bfloat16


def split_two(value):
    high = value.astype(BF16)
    low = (value - high.astype(F32)).astype(BF16)
    return high, low


def dot_f32(left, right):
    return jnp.dot(left, right, preferred_element_type=F32)


def kernel(
    count, cap, modes, cells,
    shapes_ref, weights_ref, dest_ref, cell_ref, nbr_ref, coupling_ref, inv_ref,
    state_ref, table_ref,
    tail, outgoing, arrived, loads, tag_rows, scaled, start, middle, final,
    part, sums, whole,
    send_a, recv_a, send_h, recv_h, send_g, recv_g, send_w, recv_w, state_sem,
):
    me = lax.axis_index("slab")
    nodes = dest_ref.shape[1]
    groups = LANES // cap
    width = modes // groups
    rows = COMPS * width + 16
    tall = VARS * modes
    span = cells // TILES
    step = count // TILES

    def remote(src, dst, send, recv, peer):
        return pltpu.make_async_remote_copy(
            src_ref=src, dst_ref=dst, send_sem=send, recv_sem=recv,
            device_id={"slab": peer}, device_id_type=MESH,
        )

    barrier = pltpu.get_barrier_semaphore()
    for shift in range(1, count):
        pl.semaphore_signal(
            barrier, inc=1, device_id={"slab": lax.rem(me + shift, count)}, device_id_type=MESH
        )
    for wide in (start, middle):
        wide[0] = jnp.zeros_like(wide[0])
        wide[TILES + 1] = jnp.zeros_like(wide[0])

    dest = dest_ref[...]
    height = -(-count // 16) * 16
    names = dest == lax.broadcasted_iota(jnp.int32, (height, nodes), 0)
    earlier = (
        lax.broadcasted_iota(jnp.int32, (nodes, nodes), 0)
        < lax.broadcasted_iota(jnp.int32, (nodes, nodes), 1)
    )
    before = dot_f32(names.astype(F32).astype(BF16), earlier.astype(F32).astype(BF16))
    rank = jnp.sum(jnp.where(names, before, 0.0), axis=0, keepdims=True)
    place = jnp.broadcast_to(dest.astype(F32) * LANES + rank, (8, nodes)).T[:, 0:1].astype(jnp.int32)
    lane = lax.broadcasted_iota(jnp.int32, (nodes, LANES), 1)
    tail[0 : COMPS * VARS] = weights_ref[...]
    tail[COMPS * VARS : COMPS * VARS + 1] = cell_ref[...].astype(F32)
    pieces = []
    for group in range(groups):
        taken = [
            shapes_ref[comp * modes + group * width : comp * modes + (group + 1) * width]
            for comp in range(COMPS)
        ]
        pieces.append(jnp.concatenate(taken + [tail[...]], axis=0))
    packed = jnp.concatenate(split_two(jnp.concatenate(pieces, axis=1)), axis=0)

    def pack_for(slab):
        at = place - slab * LANES
        picks = jnp.concatenate(
            [(at + group * cap == lane).astype(F32).astype(BF16) for group in range(groups)], axis=0
        )
        both = dot_f32(packed, picks)
        return both[:rows] + both[rows:]

    pl.semaphore_wait(barrier, count - 1)

    def send_step(shift, carry):
        slab = lax.rem(me + shift, count)
        outgoing[slab] = pack_for(slab)
        remote(outgoing.at[slab], arrived.at[me], send_a.at[slab], recv_a.at[me], slab).start()
        return carry

    lax.fori_loop(1, count, send_step, 0)
    arrived[me] = pack_for(me)

    filled = nbr_ref[...] >= 0
    for in_var in range(VARS):
        def scale_step(out_var, carry):
            total = inv_ref[out_var, 0:1, :] * coupling_ref[0, in_var]
            for mid in range(1, VARS):
                total = total + inv_ref[out_var, mid : mid + 1, :] * coupling_ref[mid, in_var]
            scaled[out_var, in_var] = jnp.where(filled, total, 0.0)
            return carry

        lax.fori_loop(0, VARS, scale_step, 0)

    part_of = lax.broadcasted_iota(jnp.int32, (1, LANES), 1) // cap
    depth = loads.shape[1]
    per_chunk = depth // cap
    chunks = count // per_chunk

    def take_chunk(chunk):
        for turn in range(per_chunk):
            shift = chunk * per_chunk + turn
            slab = lax.rem(me - shift + count, count)

            @pl.when(shift > 0)
            def _():
                remote(outgoing.at[slab], arrived.at[slab], send_a.at[slab], recv_a.at[slab], slab).wait_recv()

        for bunch in range(depth // LANES):
            tags = jnp.zeros((1, LANES), F32)
            built = [[None] * groups for _ in range(VARS)]
            for turn in range(groups):
                here = part_of == turn
                shift = chunk * per_chunk + bunch * groups + turn
                data = arrived[lax.rem(me - shift + count, count)]
                base = COMPS * width
                tags = jnp.where(here, data[base + 15 : base + 16], tags)
                for var in range(VARS):
                    load = data[base + COMPS * var : base + COMPS * var + 1] * data[:width]
                    for comp in range(1, COMPS):
                        at_row = base + COMPS * var + comp
                        load = load + data[at_row : at_row + 1] * data[comp * width : (comp + 1) * width]
                    for group in range(groups):
                        turn_by = ((turn - group) * cap) % LANES
                        moved = pltpu.roll(load, turn_by, 1) if turn_by else load
                        kept = built[var][group]
                        built[var][group] = moved if kept is None else jnp.where(here, moved, kept)
            at = slice(bunch * LANES, (bunch + 1) * LANES)
            for var in range(VARS):
                high, low = split_two(jnp.concatenate(built[var], axis=0))
                loads[var * modes : (var + 1) * modes, at] = high
                loads[tall + var * modes : tall + (var + 1) * modes, at] = low
            tag_rows[:, at] = jnp.broadcast_to(tags, (8, LANES))
        return tag_rows[...].T[:, 0:1].astype(jnp.int32)

    slot_cells = lax.broadcasted_iota(jnp.int32, (depth, span), 1)

    def chunk_forcing(tag_column, block):
        matches = (tag_column == slot_cells + block * span).astype(F32).astype(BF16)
        both = dot_f32(loads[...], matches)
        return both[:tall] + both[tall:]

    tag_first = take_chunk(0)

    def open_step(block, carry):
        start[block + 1] = chunk_forcing(tag_first, block)
        return carry

    lax.fori_loop(0, TILES, open_step, 0)

    def chunk_step(chunk, carry):
        tag_column = take_chunk(chunk)

        def add_step(block, carry):
            start[block + 1] = start[block + 1] + chunk_forcing(tag_column, block)
            return carry

        return lax.fori_loop(0, TILES, add_step, carry)

    lax.fori_loop(1, chunks - 1, chunk_step, 0)
    tag_last = take_chunk(chunks - 1)

    def halo(wide, turn, side):
        peer = me - 1 if side == 0 else me + 1
        near, far = (1, TILES + 1) if side == 0 else (TILES, 0)
        return remote(
            wide.at[near], wide.at[far], send_h.at[turn, side], recv_h.at[turn, 1 - side], peer
        )

    def halo_arrival(wide, turn, side):
        peer = me - 1 if side == 0 else me + 1
        near, far = (1, 0) if side == 0 else (TILES, TILES + 1)
        return remote(wide.at[near], wide.at[far], send_h.at[turn, side], recv_h.at[turn, side], peer)

    def halo_send(wide, turn):
        @pl.when(me > 0)
        def _():
            halo(wide, turn, 0).start()

        @pl.when(me < count - 1)
        def _():
            halo(wide, turn, 1).start()

    def halo_take(wide, turn):
        @pl.when(me > 0)
        def _():
            halo_arrival(wide, turn, 0).wait()

        @pl.when(me < count - 1)
        def _():
            halo_arrival(wide, turn, 1).wait()


    def begin_step(turn, carry):
        block = lax.rem(turn * (TILES - 1), TILES)
        at = pl.ds(pl.multiple_of(block * span, span), span)
        forcing = start[block + 1] + chunk_forcing(tag_last, block)
        for var in range(VARS):
            total = inv_ref[var, 0:1, at] * forcing[:modes]
            for mid in range(1, VARS):
                total = total + inv_ref[var, mid : mid + 1, at] * forcing[mid * modes : (mid + 1) * modes]
            start[block + 1, var * modes : (var + 1) * modes] = total
        return carry

    lax.fori_loop(0, 2, begin_step, 0)
    halo_send(start, 0)
    lax.fori_loop(2, TILES, begin_step, 0)

    first_cell = me * cells - span

    def sweep(wide, turn, put):
        def block_step(item, carry):
            @pl.when(item == TILES - 2)
            def _():
                halo_take(wide, turn)

            block = lax.rem(item + 1, TILES)
            for half in range(span // LANES):
                here = pl.ds(pl.multiple_of(block * span + half * LANES, LANES), LANES)
                across = slice(half * LANES, (half + 1) * LANES)
                lanes, tile = [], []
                for slot in range(NBR):
                    local = nbr_ref[slot : slot + 1, here] - (first_cell + block * span + half * LANES)
                    lanes.append(jnp.broadcast_to(jnp.bitwise_and(local, LANES - 1), (BAND, LANES)))
                    tile.append(jnp.broadcast_to(lax.shift_right_arithmetic(local, 7), (BAND, LANES)))
                for base in range(0, modes, BAND):
                    totals = [
                        start[block + 1, var * modes + base : var * modes + base + BAND, across]
                        for var in range(VARS)
                    ]
                    for slot in range(NBR):
                        for mid in range(VARS):
                            down = slice(mid * modes + base, mid * modes + base + BAND)
                            picked = None
                            for index in range(2 * span // LANES + 1):
                                at_block, at_half = divmod(half + index, span // LANES)
                                values = wide[
                                    block + at_block, down, at_half * LANES : (at_half + 1) * LANES
                                ]
                                taken = jnp.take_along_axis(
                                    values, lanes[slot], axis=1, mode="promise_in_bounds"
                                )
                                picked = taken if picked is None else jnp.where(tile[slot] == index, taken, picked)
                            for var in range(VARS):
                                totals[var] = totals[var] - scaled[var, mid, slot : slot + 1, here] * picked
                    for var in range(VARS):
                        put(block, slice(var * modes + base, var * modes + base + BAND), across, totals[var])
            return carry

        lax.fori_loop(0, TILES, block_step, 0)

    def put_middle(block, down, across, value):
        middle[block + 1, down, across] = value

    def put_final(block, down, across, value):
        high, low = split_two(value)
        final[block, down, across] = high
        final[block, slice(tall + down.start, tall + down.stop), across] = low

    sweep(start, 0, put_middle)
    halo_send(middle, 1)
    sweep(middle, 1, put_final)
    state_copy = pltpu.make_async_copy(final, state_ref, state_sem)
    state_copy.start()

    def gram_step(block, total):
        for var in range(VARS):
            stack = jnp.concatenate(
                [
                    final[block, var * modes : (var + 1) * modes],
                    final[block, tall + var * modes : tall + (var + 1) * modes],
                ],
                axis=0,
            )
            total = total + lax.dot_general(
                stack, stack, (((1,), (1,)), ((), ())), preferred_element_type=F32
            )
        return total

    gram = lax.fori_loop(0, TILES, gram_step, jnp.zeros((2 * modes, 2 * modes), F32))
    gram = gram[:modes] + gram[modes:]
    gram = gram + pltpu.roll(gram, modes, 1)
    high = modes // TILES
    for tile in range(TILES):
        owner = tile * step
        part[tile] = gram[tile * high : (tile + 1) * high]

        @pl.when(me != owner)
        def _():
            remote(part.at[tile], sums.at[me], send_g.at[tile], recv_g.at[me], owner).start()

        @pl.when(me == owner)
        def _():
            sums[me] = part[tile]

    mine = me // step

    @pl.when(lax.rem(me, step) == 0)
    def _():
        def sum_wait(shift, carry):
            slab = lax.rem(me + shift, count)
            remote(part.at[0], sums.at[slab], send_g.at[0], recv_g.at[slab], slab).wait_recv()
            return carry

        lax.fori_loop(1, count, sum_wait, 0)
        total = sums[0]
        for slab in range(1, count):
            total = total + sums[slab]
        whole[mine] = total
        for shift in range(1, count):
            slab = lax.rem(me + shift, count)
            remote(whole.at[mine], whole.at[mine], send_w.at[slab], recv_w.at[mine], slab).start()

    for tile in range(TILES):
        owner = tile * step

        @pl.when(me != owner)
        def _():
            remote(part.at[tile], sums.at[me], send_g.at[tile], recv_g.at[me], owner).wait_send()
            remote(whole.at[tile], whole.at[tile], send_w.at[0], recv_w.at[tile], owner).wait_recv()

    def sent_step(shift, carry):
        slab = lax.rem(me + shift, count)
        remote(outgoing.at[slab], arrived.at[me], send_a.at[slab], recv_a.at[me], slab).wait_send()
        return carry

    lax.fori_loop(1, count, sent_step, 0)
    table_ref[...] = jnp.concatenate([whole[tile] for tile in range(TILES)], axis=0)
    state_copy.wait()

    @pl.when(lax.rem(me, step) == 0)
    def _():
        for shift in range(1, count):
            slab = lax.rem(me + shift, count)
            remote(whole.at[mine], whole.at[mine], send_w.at[slab], recv_w.at[mine], slab).wait_send()


def finish(modes, scale, table_ref, state_ref, basis_ref, factor_ref, mixer):
    high = modes // TILES
    tall = VARS * modes

    @pl.when(pl.program_id(0) == 0)
    def _():
        row_at = lax.broadcasted_iota(jnp.int32, (modes, 2 * modes), 0)
        col_at = lax.broadcasted_iota(jnp.int32, (modes, 2 * modes), 1)
        table = table_ref[...]
        table = jnp.where(col_at < modes, table, jnp.where(col_at - modes == row_at, 1.0, 0.0))
        bands = [table[tile * high : (tile + 1) * high] for tile in range(TILES)]
        inner = lax.broadcasted_iota(jnp.int32, (high, 2 * modes), 0)
        for pivot_at in range(0, modes, GANG):
            band, offset = pivot_at // high, pivot_at % high
            columns = [
                {
                    tile: jnp.broadcast_to(bands[tile][:, pivot_at + q : pivot_at + q + 1], (high, 2 * modes))
                    for tile in range(band, TILES)
                }
                for q in range(GANG)
            ]
            rows = [bands[band][offset + q : offset + q + 1] for q in range(GANG)]
            for q in range(GANG):
                marks = [columns[q][band][offset + r : offset + r + 1] for r in range(GANG)]
                inverse = 1.0 / marks[q]
                row = rows[q] * inverse
                for r in range(q + 1, GANG):
                    ratio = marks[r] * inverse
                    for tile in range(band, TILES):
                        columns[r][tile] = columns[r][tile] - columns[q][tile] * ratio
                    rows[r] = rows[r] - marks[r] * row
                for tile in range(band, TILES):
                    column = columns[q][tile]
                    if tile == band:
                        column = jnp.where(inner > offset + q, column, 0.0)
                    bands[tile] = bands[tile] - column * row
        table = jnp.concatenate(bands, axis=0)
        diagonal = jnp.sum(jnp.where(col_at == row_at, table, 0.0), axis=1, keepdims=True)
        root = jnp.sqrt(diagonal)
        upper = jnp.where(col_at >= row_at, table * (root / diagonal) * (1.0 / scale), 0.0)
        factor_ref[...] = upper[:, :modes]
        inverse = pltpu.roll(table * (scale / root), modes, 1)[:, :modes]
        inv_high, inv_low = split_two(inverse)
        mixer[...] = jnp.concatenate([inv_high, inv_high, inv_low], axis=1)

    for var in range(VARS):
        top = state_ref[0, var * modes : (var + 1) * modes]
        bottom = state_ref[0, tall + var * modes : tall + (var + 1) * modes]
        basis_ref[var] = dot_f32(mixer[...], jnp.concatenate([top, bottom, top], axis=0))


def local(
    mode_shapes, wall_coupling, owner_dev, owner_cell, neighbours, coupling_blocks, inv_blocks
):
    count = lax.axis_size("slab")
    cells = inv_blocks.shape[2]
    nodes = mode_shapes.shape[0]
    modes = mode_shapes.shape[1] // COMPS
    cap = max(2, 2 * nodes // count)
    groups = LANES // cap
    rows = COMPS * (modes // groups) + 16
    tall = VARS * modes
    span = cells // TILES
    scale = math.sqrt(VARS * cells * count)
    vmem = pl.BlockSpec(memory_space=pltpu.VMEM)
    dma = pltpu.SemaphoreType.DMA
    state, table = pl.pallas_call(
        functools.partial(kernel, count, cap, modes, cells),
        out_shape=(
            jax.ShapeDtypeStruct((TILES, 2 * tall, span), BF16),
            jax.ShapeDtypeStruct((modes, 2 * modes), F32),
        ),
        in_specs=[vmem] * 7,
        out_specs=(pl.BlockSpec(memory_space=pl.ANY), vmem),
        scratch_shapes=[
            pltpu.VMEM((16, nodes), F32),
            pltpu.VMEM((count, rows, LANES), F32),
            pltpu.VMEM((count, rows, LANES), F32),
            pltpu.VMEM((2 * tall, 2 * LANES), BF16),
            pltpu.VMEM((8, 2 * LANES), F32),
            pltpu.VMEM((VARS, VARS, NBR, cells), F32),
            pltpu.VMEM((TILES + 2, tall, span), F32),
            pltpu.VMEM((TILES + 2, tall, span), F32),
            pltpu.VMEM((TILES, 2 * tall, span), BF16),
            pltpu.VMEM((TILES, modes // TILES, 2 * modes), F32),
            pltpu.VMEM((count, modes // TILES, 2 * modes), F32),
            pltpu.VMEM((TILES, modes // TILES, 2 * modes), F32),
            dma((count,)), dma((count,)), dma((2, 2)), dma((2, 2)),
            dma((TILES,)), dma((count,)), dma((count,)), dma((TILES,)), dma,
        ],
        compiler_params=pltpu.CompilerParams(
            collective_id=0, has_side_effects=True, vmem_limit_bytes=58 * 1024 * 1024
        ),
    )(
        mode_shapes.T, wall_coupling.T, owner_dev.T, owner_cell.reshape(1, nodes), neighbours,
        coupling_blocks.transpose(1, 2, 0, 3), inv_blocks,
    )
    return pl.pallas_call(
        functools.partial(finish, modes, scale),
        grid=(TILES,),
        out_shape=(
            jax.ShapeDtypeStruct((VARS, modes, cells), F32),
            jax.ShapeDtypeStruct((modes, modes), F32),
        ),
        in_specs=[
            pl.BlockSpec((modes, 2 * modes), lambda block: (0, 0)),
            pl.BlockSpec((1, 2 * tall, span), lambda block: (block, 0, 0)),
        ],
        out_specs=(
            pl.BlockSpec((VARS, modes, span), lambda block: (0, 0, block)),
            pl.BlockSpec((modes, modes), lambda block: (0, 0)),
        ),
        scratch_shapes=[pltpu.VMEM((modes, 3 * modes), BF16)],
    )(table, state)


def solution(mesh):
    in_specs = (
        P(("groups", "slab"), None),
        P(("groups", "slab"), None),
        P(("groups", "slab"), None),
        P(("groups", "slab")),
        P(None, ("groups", "slab")),
        P(None, None, None, ("groups", "slab")),
        P(None, None, ("groups", "slab")),
    )
    out_specs = (P(None, None, ("groups", "slab")), P("groups", None))
    return jax.shard_map(local, mesh=mesh, in_specs=in_specs, out_specs=out_specs, check_vma=False)
```

```python
import functools
import math

import jax
import jax.numpy as jnp
from jax import lax
from jax.experimental import pallas as pl
from jax.experimental.pallas import tpu as pltpu
from jax.sharding import PartitionSpec as P

VARS = 5
NBR = 6
BY_MATMUL = 4
COMPS = 3
LANES = 128
TILES = 8
BAND = 32
GANG = 8
MESH = pl.DeviceIdType.MESH
F32 = jnp.float32
BF16 = jnp.bfloat16


def split_two(value):
    high = value.astype(BF16)
    low = (value - high.astype(F32)).astype(BF16)
    return high, low


def dot_f32(left, right):
    return jnp.dot(left, right, preferred_element_type=F32)


def kernel(
    count, cap, modes, cells,
    shapes_ref, weights_ref, dest_ref, cell_ref, nbr_ref, coupling_ref, inv_ref,
    state_ref, table_ref,
    tail, outgoing, arrived, loads, tag_rows, hot, scaled, start, middle, first, second, even, odd,
    part, sums, whole,
    send_a, recv_a, send_h, recv_h, send_g, recv_g, send_w, recv_w, state_sem,
):
    me = lax.axis_index("slab")
    nodes = dest_ref.shape[1]
    groups = LANES // cap
    width = modes // groups
    rows = COMPS * width + 16
    tall = VARS * modes
    span = cells // TILES
    step = count // TILES

    def remote(src, dst, send, recv, peer):
        return pltpu.make_async_remote_copy(
            src_ref=src, dst_ref=dst, send_sem=send, recv_sem=recv,
            device_id={"slab": peer}, device_id_type=MESH,
        )

    barrier = pltpu.get_barrier_semaphore()
    for shift in range(1, count):
        pl.semaphore_signal(
            barrier, inc=1, device_id={"slab": lax.rem(me + shift, count)}, device_id_type=MESH
        )
    for wide in (start, middle):
        wide[0] = jnp.zeros_like(wide[0])
        wide[TILES + 1] = jnp.zeros_like(wide[0])

    dest = dest_ref[...]
    height = -(-count // 16) * 16
    names = dest == lax.broadcasted_iota(jnp.int32, (height, nodes), 0)
    earlier = (
        lax.broadcasted_iota(jnp.int32, (nodes, nodes), 0)
        < lax.broadcasted_iota(jnp.int32, (nodes, nodes), 1)
    )
    before = dot_f32(names.astype(F32).astype(BF16), earlier.astype(F32).astype(BF16))
    rank = jnp.sum(jnp.where(names, before, 0.0), axis=0, keepdims=True)
    place = jnp.broadcast_to(dest.astype(F32) * LANES + rank, (8, nodes)).T[:, 0:1].astype(jnp.int32)
    lane = lax.broadcasted_iota(jnp.int32, (nodes, LANES), 1)
    tail[0 : COMPS * VARS] = weights_ref[...]
    tail[COMPS * VARS : COMPS * VARS + 1] = cell_ref[...].astype(F32)
    pieces = []
    for group in range(groups):
        taken = [
            shapes_ref[comp * modes + group * width : comp * modes + (group + 1) * width]
            for comp in range(COMPS)
        ]
        pieces.append(jnp.concatenate(taken + [tail[...]], axis=0))
    packed = jnp.concatenate(split_two(jnp.concatenate(pieces, axis=1)), axis=0)

    def pack_for(slab):
        at = place - slab * LANES
        picks = jnp.concatenate(
            [(at + group * cap == lane).astype(F32).astype(BF16) for group in range(groups)], axis=0
        )
        both = dot_f32(packed, picks)
        return both[:rows] + both[rows:]

    pl.semaphore_wait(barrier, count - 1)

    def send_step(shift, carry):
        slab = lax.rem(me + shift, count)
        outgoing[slab] = pack_for(slab)
        remote(outgoing.at[slab], arrived.at[me], send_a.at[slab], recv_a.at[me], slab).start()
        return carry

    lax.fori_loop(1, count, send_step, 0)
    arrived[me] = pack_for(me)

    first_cell = me * cells - span
    window = lax.broadcasted_iota(jnp.int32, (3 * span, span), 0)

    def hot_step(block, carry):
        at = pl.ds(pl.multiple_of(block * span, span), span)
        for slot in range(BY_MATMUL):
            names_now = nbr_ref[slot : slot + 1, at]
            local = jnp.where(names_now >= 0, names_now - (first_cell + block * span), -1)
            hot[block, :, slot * span : (slot + 1) * span] = (window == local).astype(F32).astype(BF16)
        return carry

    lax.fori_loop(0, TILES, hot_step, 0)

    filled = nbr_ref[...] >= 0
    for in_var in range(VARS):
        def scale_step(out_var, carry):
            total = inv_ref[out_var, 0:1, :] * coupling_ref[0, in_var]
            for mid in range(1, VARS):
                total = total + inv_ref[out_var, mid : mid + 1, :] * coupling_ref[mid, in_var]
            scaled[out_var, in_var] = jnp.where(filled, total, 0.0)
            return carry

        lax.fori_loop(0, VARS, scale_step, 0)

    part_of = lax.broadcasted_iota(jnp.int32, (1, LANES), 1) // cap
    depth = loads.shape[1]
    per_chunk = depth // cap
    chunks = count // per_chunk

    def take_chunk(chunk):
        for turn in range(per_chunk):
            shift = chunk * per_chunk + turn
            slab = lax.rem(me - shift + count, count)

            @pl.when(shift > 0)
            def _():
                remote(outgoing.at[slab], arrived.at[slab], send_a.at[slab], recv_a.at[slab], slab).wait_recv()

        for bunch in range(depth // LANES):
            tags = jnp.zeros((1, LANES), F32)
            built = [[None] * groups for _ in range(VARS)]
            for turn in range(groups):
                here = part_of == turn
                shift = chunk * per_chunk + bunch * groups + turn
                data = arrived[lax.rem(me - shift + count, count)]
                base = COMPS * width
                tags = jnp.where(here, data[base + 15 : base + 16], tags)
                for var in range(VARS):
                    load = data[base + COMPS * var : base + COMPS * var + 1] * data[:width]
                    for comp in range(1, COMPS):
                        at_row = base + COMPS * var + comp
                        load = load + data[at_row : at_row + 1] * data[comp * width : (comp + 1) * width]
                    for group in range(groups):
                        turn_by = ((turn - group) * cap) % LANES
                        moved = pltpu.roll(load, turn_by, 1) if turn_by else load
                        kept = built[var][group]
                        built[var][group] = moved if kept is None else jnp.where(here, moved, kept)
            at = slice(bunch * LANES, (bunch + 1) * LANES)
            for var in range(VARS):
                high, low = split_two(jnp.concatenate(built[var], axis=0))
                loads[var * modes : (var + 1) * modes, at] = high
                loads[tall + var * modes : tall + (var + 1) * modes, at] = low
            tag_rows[:, at] = jnp.broadcast_to(tags, (8, LANES))
        return tag_rows[...].T[:, 0:1].astype(jnp.int32)

    slot_cells = lax.broadcasted_iota(jnp.int32, (depth, span), 1)

    def chunk_forcing(tag_column, block):
        matches = (tag_column == slot_cells + block * span).astype(F32).astype(BF16)
        both = dot_f32(loads[...], matches)
        return both[:tall] + both[tall:]

    tag_first = take_chunk(0)

    def open_step(block, carry):
        start[block + 1] = chunk_forcing(tag_first, block)
        return carry

    lax.fori_loop(0, TILES, open_step, 0)

    def chunk_step(chunk, carry):
        tag_column = take_chunk(chunk)

        def add_step(block, carry):
            start[block + 1] = start[block + 1] + chunk_forcing(tag_column, block)
            return carry

        return lax.fori_loop(0, TILES, add_step, carry)

    lax.fori_loop(1, chunks - 1, chunk_step, 0)
    tag_last = take_chunk(chunks - 1)

    def keep(state, block, var, value):
        high, low = split_two(value)
        state[block + 1, var * modes : (var + 1) * modes] = high
        state[block + 1, tall + var * modes : tall + (var + 1) * modes] = low

    def halo(wide, turn, side):
        peer = me - 1 if side == 0 else me + 1
        near, far = (1, TILES + 1) if side == 0 else (TILES, 0)
        return remote(
            wide.at[near], wide.at[far], send_h.at[turn, side], recv_h.at[turn, 1 - side], peer
        )

    def halo_arrival(wide, turn, side):
        peer = me - 1 if side == 0 else me + 1
        near, far = (1, 0) if side == 0 else (TILES, TILES + 1)
        return remote(wide.at[near], wide.at[far], send_h.at[turn, side], recv_h.at[turn, side], peer)

    def halo_send(wide, turn):
        @pl.when(me > 0)
        def _():
            halo(wide, turn, 0).start()

        @pl.when(me < count - 1)
        def _():
            halo(wide, turn, 1).start()

    def halo_take(wide, turn, state):
        @pl.when(me > 0)
        def _():
            halo_arrival(wide, turn, 0).wait()

        @pl.when(me < count - 1)
        def _():
            halo_arrival(wide, turn, 1).wait()

        for block in (-1, TILES):
            for var in range(VARS):
                keep(state, block, var, wide[block + 1, var * modes : (var + 1) * modes])

    def begin_step(turn, carry):
        block = lax.rem(turn * (TILES - 1), TILES)
        at = pl.ds(pl.multiple_of(block * span, span), span)
        forcing = start[block + 1] + chunk_forcing(tag_last, block)
        for var in range(VARS):
            total = inv_ref[var, 0:1, at] * forcing[:modes]
            for mid in range(1, VARS):
                total = total + inv_ref[var, mid : mid + 1, at] * forcing[mid * modes : (mid + 1) * modes]
            start[block + 1, var * modes : (var + 1) * modes] = total
            keep(first, block, var, total)
        return carry

    lax.fori_loop(0, 2, begin_step, 0)
    halo_send(start, 0)
    lax.fori_loop(2, TILES, begin_step, 0)

    def gather(source, gathered, block):
        near = jnp.concatenate([source[block], source[block + 1], source[block + 2]], axis=1)
        for slot in range(BY_MATMUL):
            both = dot_f32(near, hot[block, :, slot * span : (slot + 1) * span])
            gathered[slot] = both[:tall] + both[tall:]

    def mix(gathered, wide, target, kept, block):
        for half in range(span // LANES):
            here = pl.ds(pl.multiple_of(block * span + half * LANES, LANES), LANES)
            across = slice(half * LANES, (half + 1) * LANES)
            lanes, tile = {}, {}
            for slot in range(BY_MATMUL, NBR):
                local = nbr_ref[slot : slot + 1, here] - (first_cell + block * span + half * LANES)
                lanes[slot] = jnp.broadcast_to(jnp.bitwise_and(local, LANES - 1), (BAND, LANES))
                tile[slot] = jnp.broadcast_to(lax.shift_right_arithmetic(local, 7), (BAND, LANES))
            for base in range(0, modes, BAND):
                totals = [
                    start[block + 1, var * modes + base : var * modes + base + BAND, across]
                    for var in range(VARS)
                ]
                for slot in range(NBR):
                    for mid in range(VARS):
                        down = slice(mid * modes + base, mid * modes + base + BAND)
                        if slot < BY_MATMUL:
                            picked = gathered[slot, down, across]
                        else:
                            picked = None
                            for index in range(2 * span // LANES + 1):
                                at_block, at_half = divmod(half + index, span // LANES)
                                values = wide[
                                    block + at_block, down, at_half * LANES : (at_half + 1) * LANES
                                ]
                                taken = jnp.take_along_axis(
                                    values, lanes[slot], axis=1, mode="promise_in_bounds"
                                )
                                picked = taken if picked is None else jnp.where(tile[slot] == index, taken, picked)
                        for var in range(VARS):
                            totals[var] = totals[var] - scaled[var, mid, slot : slot + 1, here] * picked
                for var in range(VARS):
                    rows_at = slice(var * modes + base, var * modes + base + BAND)
                    low_at = slice(tall + var * modes + base, tall + var * modes + base + BAND)
                    high, low = split_two(totals[var])
                    target[block + 1, rows_at, across] = high
                    target[block + 1, low_at, across] = low
                    if kept is not None:
                        kept[block + 1, rows_at, across] = totals[var]

    def sweep(source, wide, target, kept, turn):
        def block_of(item):
            return lax.rem(item + 1, TILES)

        gather(source, even, block_of(0))

        def pair_step(pair, carry):
            @pl.when(pair == TILES // 2 - 2)
            def _():
                halo_take(wide, turn, source)

            item = 2 * pair
            gather(source, odd, block_of(item + 1))
            mix(even, wide, target, kept, block_of(item))
            gather(source, even, block_of(item + 2))
            mix(odd, wide, target, kept, block_of(item + 1))
            return carry

        lax.fori_loop(0, TILES // 2 - 1, pair_step, 0)
        gather(source, odd, 0)
        mix(even, wide, target, kept, TILES - 1)
        mix(odd, wide, target, kept, 0)

    sweep(first, start, second, middle, 0)
    halo_send(middle, 1)
    sweep(second, middle, first, None, 1)
    state_copy = pltpu.make_async_copy(first.at[pl.ds(1, TILES)], state_ref, state_sem)
    state_copy.start()

    def gram_step(block, total):
        for var in range(VARS):
            stack = jnp.concatenate(
                [
                    first[block + 1, var * modes : (var + 1) * modes],
                    first[block + 1, tall + var * modes : tall + (var + 1) * modes],
                ],
                axis=0,
            )
            total = total + lax.dot_general(
                stack, stack, (((1,), (1,)), ((), ())), preferred_element_type=F32
            )
        return total

    gram = lax.fori_loop(0, TILES, gram_step, jnp.zeros((2 * modes, 2 * modes), F32))
    gram = gram[:modes] + gram[modes:]
    gram = gram + pltpu.roll(gram, modes, 1)
    high = modes // TILES
    for tile in range(TILES):
        owner = tile * step
        part[tile] = gram[tile * high : (tile + 1) * high]

        @pl.when(me != owner)
        def _():
            remote(part.at[tile], sums.at[me], send_g.at[tile], recv_g.at[me], owner).start()

        @pl.when(me == owner)
        def _():
            sums[me] = part[tile]

    mine = me // step

    @pl.when(lax.rem(me, step) == 0)
    def _():
        def sum_wait(shift, carry):
            slab = lax.rem(me + shift, count)
            remote(part.at[0], sums.at[slab], send_g.at[0], recv_g.at[slab], slab).wait_recv()
            return carry

        lax.fori_loop(1, count, sum_wait, 0)
        total = sums[0]
        for slab in range(1, count):
            total = total + sums[slab]
        whole[mine] = total
        for shift in range(1, count):
            slab = lax.rem(me + shift, count)
            remote(whole.at[mine], whole.at[mine], send_w.at[slab], recv_w.at[mine], slab).start()

    for tile in range(TILES):
        owner = tile * step

        @pl.when(me != owner)
        def _():
            remote(part.at[tile], sums.at[me], send_g.at[tile], recv_g.at[me], owner).wait_send()
            remote(whole.at[tile], whole.at[tile], send_w.at[0], recv_w.at[tile], owner).wait_recv()

    def sent_step(shift, carry):
        slab = lax.rem(me + shift, count)
        remote(outgoing.at[slab], arrived.at[me], send_a.at[slab], recv_a.at[me], slab).wait_send()
        return carry

    lax.fori_loop(1, count, sent_step, 0)
    table_ref[...] = jnp.concatenate([whole[tile] for tile in range(TILES)], axis=0)
    state_copy.wait()

    @pl.when(lax.rem(me, step) == 0)
    def _():
        for shift in range(1, count):
            slab = lax.rem(me + shift, count)
            remote(whole.at[mine], whole.at[mine], send_w.at[slab], recv_w.at[mine], slab).wait_send()


def finish(modes, scale, table_ref, state_ref, basis_ref, factor_ref, mixer):
    high = modes // TILES
    tall = VARS * modes

    @pl.when(pl.program_id(0) == 0)
    def _():
        row_at = lax.broadcasted_iota(jnp.int32, (modes, 2 * modes), 0)
        col_at = lax.broadcasted_iota(jnp.int32, (modes, 2 * modes), 1)
        table = table_ref[...]
        table = jnp.where(col_at < modes, table, jnp.where(col_at - modes == row_at, 1.0, 0.0))
        bands = [table[tile * high : (tile + 1) * high] for tile in range(TILES)]
        inner = lax.broadcasted_iota(jnp.int32, (high, 2 * modes), 0)
        for pivot_at in range(0, modes, GANG):
            band, offset = pivot_at // high, pivot_at % high
            columns = [
                {
                    tile: jnp.broadcast_to(bands[tile][:, pivot_at + q : pivot_at + q + 1], (high, 2 * modes))
                    for tile in range(band, TILES)
                }
                for q in range(GANG)
            ]
            rows = [bands[band][offset + q : offset + q + 1] for q in range(GANG)]
            for q in range(GANG):
                marks = [columns[q][band][offset + r : offset + r + 1] for r in range(GANG)]
                inverse = 1.0 / marks[q]
                row = rows[q] * inverse
                for r in range(q + 1, GANG):
                    ratio = marks[r] * inverse
                    for tile in range(band, TILES):
                        columns[r][tile] = columns[r][tile] - columns[q][tile] * ratio
                    rows[r] = rows[r] - marks[r] * row
                for tile in range(band, TILES):
                    column = columns[q][tile]
                    if tile == band:
                        column = jnp.where(inner > offset + q, column, 0.0)
                    bands[tile] = bands[tile] - column * row
        table = jnp.concatenate(bands, axis=0)
        diagonal = jnp.sum(jnp.where(col_at == row_at, table, 0.0), axis=1, keepdims=True)
        root = jnp.sqrt(diagonal)
        upper = jnp.where(col_at >= row_at, table * (root / diagonal) * (1.0 / scale), 0.0)
        factor_ref[...] = upper[:, :modes]
        inverse = pltpu.roll(table * (scale / root), modes, 1)[:, :modes]
        inv_high, inv_low = split_two(inverse)
        mixer[...] = jnp.concatenate([inv_high, inv_high, inv_low], axis=1)

    for var in range(VARS):
        top = state_ref[0, var * modes : (var + 1) * modes]
        bottom = state_ref[0, tall + var * modes : tall + (var + 1) * modes]
        basis_ref[var] = dot_f32(mixer[...], jnp.concatenate([top, bottom, top], axis=0))


def local(
    mode_shapes, wall_coupling, owner_dev, owner_cell, neighbours, coupling_blocks, inv_blocks
):
    count = lax.axis_size("slab")
    cells = inv_blocks.shape[2]
    nodes = mode_shapes.shape[0]
    modes = mode_shapes.shape[1] // COMPS
    cap = max(2, 2 * nodes // count)
    groups = LANES // cap
    rows = COMPS * (modes // groups) + 16
    tall = VARS * modes
    span = cells // TILES
    scale = math.sqrt(VARS * cells * count)
    vmem = pl.BlockSpec(memory_space=pltpu.VMEM)
    dma = pltpu.SemaphoreType.DMA
    state, table = pl.pallas_call(
        functools.partial(kernel, count, cap, modes, cells),
        out_shape=(
            jax.ShapeDtypeStruct((TILES, 2 * tall, span), BF16),
            jax.ShapeDtypeStruct((modes, 2 * modes), F32),
        ),
        in_specs=[vmem] * 7,
        out_specs=(pl.BlockSpec(memory_space=pl.ANY), vmem),
        scratch_shapes=[
            pltpu.VMEM((16, nodes), F32),
            pltpu.VMEM((count, rows, LANES), F32),
            pltpu.VMEM((count, rows, LANES), F32),
            pltpu.VMEM((2 * tall, 2 * LANES), BF16),
            pltpu.VMEM((8, 2 * LANES), F32),
            pltpu.VMEM((TILES, 3 * span, BY_MATMUL * span), BF16),
            pltpu.VMEM((VARS, VARS, NBR, cells), F32),
            pltpu.VMEM((TILES + 2, tall, span), F32),
            pltpu.VMEM((TILES + 2, tall, span), F32),
            pltpu.VMEM((TILES + 2, 2 * tall, span), BF16),
            pltpu.VMEM((TILES + 2, 2 * tall, span), BF16),
            pltpu.VMEM((BY_MATMUL, tall, span), F32),
            pltpu.VMEM((BY_MATMUL, tall, span), F32),
            pltpu.VMEM((TILES, modes // TILES, 2 * modes), F32),
            pltpu.VMEM((count, modes // TILES, 2 * modes), F32),
            pltpu.VMEM((TILES, modes // TILES, 2 * modes), F32),
            dma((count,)), dma((count,)), dma((2, 2)), dma((2, 2)),
            dma((TILES,)), dma((count,)), dma((count,)), dma((TILES,)), dma,
        ],
        compiler_params=pltpu.CompilerParams(
            collective_id=0, has_side_effects=True, vmem_limit_bytes=58 * 1024 * 1024
        ),
    )(
        mode_shapes.T, wall_coupling.T, owner_dev.T, owner_cell.reshape(1, nodes), neighbours,
        coupling_blocks.transpose(1, 2, 0, 3), inv_blocks,
    )
    return pl.pallas_call(
        functools.partial(finish, modes, scale),
        grid=(TILES,),
        out_shape=(
            jax.ShapeDtypeStruct((VARS, modes, cells), F32),
            jax.ShapeDtypeStruct((modes, modes), F32),
        ),
        in_specs=[
            pl.BlockSpec((modes, 2 * modes), lambda block: (0, 0)),
            pl.BlockSpec((1, 2 * tall, span), lambda block: (block, 0, 0)),
        ],
        out_specs=(
            pl.BlockSpec((VARS, modes, span), lambda block: (0, 0, block)),
            pl.BlockSpec((modes, modes), lambda block: (0, 0)),
        ),
        scratch_shapes=[pltpu.VMEM((modes, 3 * modes), BF16)],
    )(table, state)


def solution(mesh):
    in_specs = (
        P(("groups", "slab"), None),
        P(("groups", "slab"), None),
        P(("groups", "slab"), None),
        P(("groups", "slab")),
        P(None, ("groups", "slab")),
        P(None, None, None, ("groups", "slab")),
        P(None, None, ("groups", "slab")),
    )
    out_specs = (P(None, None, ("groups", "slab")), P("groups", None))
    return jax.shard_map(local, mesh=mesh, in_specs=in_specs, out_specs=out_specs, check_vma=False)
```
